256 devices in a mesh: tensor: 2 (over x_hi), shard: 16 (over z, x_lo), replica: 8 (over y, core).
Axes of the slice: x: 4 (x_hi: 2, x_lo: 2; x = x_hi * 2 + x_lo), y: 4, z: 8, core: 2. Of those that a mesh axis runs over, the one named last changes fastest.
Arguments:
- activations: bfloat16 [32768, 16384], P(('shard', 'replica'), 'tensor'), may hold values from -24 to 24
- value_cotangent: bfloat16 [32768, 512], P(('shard', 'replica')), may hold values from -0.03125 to 0.03125
- key_gradient: float32 [16384, 512], P('shard', 'tensor'), may hold values from -6 to 6
- key_master: float32 [16384, 512], P('shard', 'tensor'), may hold values from -6 to 6
- key_moment: float32 [16384, 512], P('shard', 'tensor'), may hold values from -6 to 6
- key_second: float32 [16384, 512], P('shard', 'tensor'), may hold values from 0.01 to 1
- step_count: int32 [1], replicated, may hold values from 1 to 9
- previous_value: bfloat16 [16384, 512], P(('tensor', 'shard')), may hold values from -0.25 to 0.25
- previous_cotangent: bfloat16 [32768, 512], P(('shard', 'replica'), 'tensor'), may hold values from -6 to 6
Outputs:
- value_grad: float32 [16384, 512], P(('tensor', 'shard'))
- moment_new: float32 [16384, 512], P('shard', 'tensor')
- second_new: float32 [16384, 512], P('shard', 'tensor')
- key_update: float32 [16384, 512], P('shard', 'tensor')
- input_grad: bfloat16 [32768, 16384], P(('shard', 'replica'), 'tensor')
The draws below stay inside these ranges and needn't reach their ends.
All inputs are finite; a program needn't handle non-finite values.
Results may differ from the reference program's by a relative error of at most 0.001.
Values may be sent and summed in bfloat16 or wider, within the bound.
A program may use at most 192 MiB of HBM per device.

```python
import math
import jax
import jax.numpy as jnp
from jax import lax

D = 16384
C1 = 512
C2 = 512
C3 = 512
TOKENS = 32768


def raised(drawn, key, source, target, shards_of, factor):
    def block_of(position):
        return (jnp.arange(drawn.shape[position]) // (drawn.shape[position] // shards_of)).reshape((-1,) + (1,) * (drawn.ndim - 1 - position))

    first = jax.random.permutation(key, shards_of)[block_of(target)]
    second = (block_of(target) + shards_of // 2) % shards_of
    return jnp.where((block_of(source) == first) | (block_of(source) == second), factor * drawn, drawn)


def level_of(own_key, dims, split, smallest, largest):
    gain, own = 1.0, jax.random.fold_in(own_key, 6)
    for axis_at, parts in split:
        heights = jnp.exp(jax.random.uniform(jax.random.fold_in(own, axis_at), (parts,), jnp.float32, smallest / len(split), largest / len(split)))
        gain = gain * jnp.repeat(heights, dims[axis_at] // parts).reshape([-1 if axis == axis_at else 1 for axis in range(len(dims))])
    return gain


def scatter_about(rng, extent, deviation, most, shards=(), dtype=jnp.bfloat16):
    level = level_of(rng, extent, shards, -0.22, 0.18) if shards else 1.0
    result = jax.random.normal(rng, extent, jnp.float32) * deviation * level
    return jnp.minimum(jnp.maximum(result, -most), most).astype(dtype)


def gaussian_with(key, dims, scale, most, shards, heavy, dtype=jnp.bfloat16):
    result = scale * jax.random.normal(key, dims, jnp.float32)
    if shards:
        result = result * level_of(key, dims, shards, -0.22, 0.18)
    return jnp.clip(raised(result, jax.random.fold_in(key, 3), *heavy), -most, most).astype(dtype)


def setup_inputs(seed: int = 0) -> dict:
    seeds = jax.random.split(jax.random.key(seed), 10)
    activations = gaussian_with(seeds[0], (TOKENS, D), 1.0, 24.0, ((0, 128), (1, 2)), (0, 1, 128, 5.5))
    value_cotangent = scatter_about(seeds[1], (TOKENS, C1), TOKENS ** -0.5, 0.03125, ((0, 128),))
    key_gradient = scatter_about(seeds[2], (D, C2), 1.0, 6.0, ((0, 16), (1, 2)), jnp.float32)
    key_master = scatter_about(seeds[3], (D, C2), 2.0, 6.0, ((0, 16), (1, 2)), jnp.float32)
    key_moment = scatter_about(seeds[4], (D, C2), 1.0, 6.0, ((0, 16), (1, 2)), jnp.float32)
    key_second = jnp.clip(jnp.exp(math.log(1.0) - 4.6051702 * jax.random.uniform(seeds[5], (D, C2), jnp.float32) ** level_of(seeds[5], (D, C2), ((0, 16), (1, 2)), -0.2, 0.2)), 0.01, 1.0)
    step_count = jax.random.randint(seeds[6], (1,), 1, 10).astype(jnp.int32)
    previous_value = scatter_about(seeds[7], (D, C3), C3 ** -0.5, 0.25, ((0, 32),))
    previous_cotangent = scatter_about(seeds[8], (TOKENS, C3), 1.0, 6.0, ((0, 128), (1, 2)))
    return {"activations": activations, "value_cotangent": value_cotangent, "key_gradient": key_gradient, "key_master": key_master, "key_moment": key_moment, "key_second": key_second, "step_count": step_count, "previous_value": previous_value, "previous_cotangent": previous_cotangent}


def reference(activations, value_cotangent, key_gradient, key_master, key_moment, key_second, step_count, previous_value, previous_cotangent):
    value_grad = lax.dot_general(activations, value_cotangent, (((0,), (0,)), ((), ())), preferred_element_type=jnp.float32)
    moment_new = 0.9 * key_moment + 0.1 * key_gradient
    second_new = 0.95 * key_second + 0.05 * key_gradient * key_gradient
    steps_done = step_count.astype(jnp.float32)[0]
    first_fix = 1.0 - jnp.power(jnp.float32(0.9), steps_done)
    second_fix = 1.0 - jnp.power(jnp.float32(0.95), steps_done)
    key_update = moment_new / first_fix / (jnp.sqrt(second_new / second_fix) + 1e-08) + 0.1 * key_master
    input_grad = lax.dot_general(previous_cotangent, previous_value, (((1,), (1,)), ((), ())), preferred_element_type=jnp.float32).astype(jnp.bfloat16)
    return (value_grad, moment_new, second_new, key_update, input_grad)
```

```python
import functools

import jax
import jax.numpy as jnp
from jax import lax
from jax.experimental import pallas as pl
from jax.experimental.pallas import tpu as pltpu
from jax.sharding import PartitionSpec as P

MESH = pl.DeviceIdType.MESH
F32, BF16, I16, I32 = jnp.float32, jnp.bfloat16, jnp.int16, jnp.int32
Z, Y = 8, 4
TOK, FEAT, COLS = 256, 8192, 512
HALF = 256
QUARTER = COLS // Y
STEPS = 12
HOPS = {1: (4, 3, 4), -1: (3, 4, 3)}


def coded(x):
    top = jnp.maximum(jnp.max(jnp.abs(x), axis=0, keepdims=True), 1e-30)
    return jnp.round(x * (32767.0 / top)).astype(I32).astype(I16), top * (1.0 / 32767.0)


def plain(q, scale):
    return q.astype(I32).astype(F32) * scale


def exchange(
    acts, g, pv, pc,
    w, cot, fin, fin_scale,
    a_own, a_par, g_buf, g_t, part,
    m1s, m1r, m1ss, m1sr, m2s, m2r, m2ss, m2sr,
    xs, xr, xss, xsr, zs, zr, zss, zsr,
    a_local, a_send, a_recv, one, w_recv, w_pair_recv, w_ring_send, w_x_send, w_pair_send,
    m1_send, m1_recv, m2_send, m2_recv, x_send, x_recv, z_send, z_recv, f_send, f_recv, fp_send, fp_recv,
):
    tensor = lax.axis_index("tensor")
    shard = lax.axis_index("shard")
    replica = lax.axis_index("replica")
    z, x = shard // 2, shard % 2
    y, core = replica // 2, replica % 2
    sgn = 1 - 2 * core

    def ring(at, n):
        return lax.rem(at + 2 * n, n)

    to_pair = (tensor, shard, y * 2 + 1 - core)
    to_x = (tensor, z * 2 + 1 - x, replica)
    to_tensor = (1 - tensor, shard, replica)

    def to_y(r):
        return (tensor, shard, ring(y + r, Y) * 2 + core)

    def to_z(way):
        return (tensor, ring(z + way * sgn, Z) * 2 + x, replica)

    def remote(src, dst, send, recv, device):
        return pltpu.make_async_remote_copy(
            src_ref=src, dst_ref=dst, send_sem=send, recv_sem=recv, device_id=device, device_id_type=MESH
        )

    barrier = pltpu.get_barrier_semaphore()
    peers = (to_pair, to_x, to_tensor, to_y(1), to_y(2), to_y(3), to_z(1), to_z(-1))
    for peer in peers:
        pl.semaphore_signal(barrier, inc=1, device_id=peer, device_id_type=MESH)
    pl.semaphore_wait(barrier, len(peers))

    def columns(t, b, of_core):
        far = Z // 2 - (t + 1) // 2
        offset = jnp.where(t % 2 == 1, far, -far) * (1 - 2 * of_core)
        start = (ring(z + offset, Z) * 2 + b) * 2 * HALF + of_core * HALF
        return pl.ds(pl.multiple_of(start, HALF), HALF)

    def own_acts(t, b):
        return pltpu.make_async_copy(
            acts.at[:, columns(t, b, core)], a_own.at[t, :, pl.ds(b * HALF, HALF)], a_local.at[t, b]
        )

    def pair_acts(t, b):
        return remote(
            acts.at[:, columns(t, b, 1 - core)], a_par.at[t, :, pl.ds(b * HALF, HALF)],
            a_send.at[t, b], a_recv.at[t, b], to_pair,
        )

    own_g = pltpu.make_async_copy(g, g_buf.at[0], one.at[0])
    pair_g = remote(g, g_buf.at[1], one.at[1], one.at[2], to_pair)
    own_w = pltpu.make_async_copy(pv, w.at[pl.ds(pl.multiple_of(shard * 4, 4), 4)], one.at[3])
    own_cot = pltpu.make_async_copy(pc, cot.at[:, pl.ds(pl.multiple_of(tensor * 256, 256), 256)], one.at[4])
    pair_cot = remote(pc, cot.at[:, pl.ds(pl.multiple_of(tensor * 256, 256), 256)], one.at[5], one.at[6], to_tensor)

    def slot(zo, xo, half, of_core):
        return ((zo * 2 + xo) * 2 + of_core) * 2 + half

    def mark(zo, xo, half):
        return (zo * 2 + xo) * 2 + half

    def flow_of(flow):
        return (1 - x if flow == 1 else x), (1 if flow == 2 else 0)

    def origin(way, k):
        return ring(z - way * sgn * k, Z)

    def ring_copy(flow, way, k):
        xo, half = flow_of(flow)
        zo = origin(way, k)
        at = w.at[slot(zo, xo, half, core)]
        return remote(at, at, w_ring_send.at[0 if way == 1 else 1, flow * 4 + k], w_recv.at[mark(zo, xo, half)], to_z(way))

    def x_copy(zo, half, k):
        at = w.at[slot(zo, x, half, core)]
        return remote(at, at, w_x_send.at[k], w_recv.at[mark(zo, x, half)], to_x)

    def pair_copy(zo, xo, half):
        at = w.at[slot(zo, xo, half, core)]
        return remote(at, at, w_pair_send.at[mark(zo, xo, half)], w_pair_recv.at[mark(zo, xo, half)], to_pair)

    def arrive(zo, xo, half):
        at = w.at[slot(zo, xo, half, core)]
        remote(at, at, w_x_send.at[0], w_recv.at[mark(zo, xo, half)], to_x).wait_recv()

    def x_index(way, k):
        return 2 * k + (0 if way == 1 else 1)

    def ring_event(flow, way, k):
        xo, half = flow_of(flow)
        zo = origin(way, k)
        arrive(zo, xo, half)

        @pl.when(k < HOPS[way][flow])
        def _():
            ring_copy(flow, way, k).start()

        if flow == 2:
            x_copy(zo, half, x_index(way, k)).start()
        pair_copy(zo, xo, half).start()

    def x_event(way, k):
        zo = origin(way, k)
        arrive(zo, 1 - x, 1)
        pair_copy(zo, 1 - x, 1).start()

    own_g.start()
    pair_g.start()
    own_w.start()

    def start_acts(t, carry):
        for b in range(2):
            own_acts(t, b).start()
            pair_acts(t, b).start()
        return carry

    lax.fori_loop(0, 1, start_acts, 0)
    own_w.wait()
    x_copy(z, 0, 0).start()
    for way in (1, -1):
        ring_copy(0, way, 0).start()
    x_copy(z, 1, 1).start()
    for way in (1, -1):
        ring_copy(2, way, 0).start()
    lax.fori_loop(1, Z, start_acts, 0)
    own_cot.start()
    pair_cot.start()

    own_g.wait()
    pair_g.wait_recv()
    for r in range(Y):
        take = pl.ds(pl.multiple_of(ring(y + r, Y) * QUARTER, QUARTER), QUARTER)
        for b in range(2):
            g_t[r * QUARTER : (r + 1) * QUARTER, b * TOK : (b + 1) * TOK] = (
                g_buf[b, :, take].astype(F32).T.astype(BF16)
            )

    A, B = slice(0, QUARTER // 2), slice(QUARTER // 2, QUARTER)
    half_rows = QUARTER // 2

    def rows(r, first=0, count=QUARTER):
        return pl.ds(r * QUARTER + first, count)

    def along_y(src, dst, src_scale, dst_scale, send, recv, t, way):
        to = to_y(1 if way == 0 else 3)
        return (
            remote(src.at[t, way], dst.at[t, way], send.at[t, way, 0], recv.at[t, way, 0], to),
            remote(src_scale.at[t, way], dst_scale.at[t, way], send.at[t, way, 1], recv.at[t, way, 1], to),
        )

    m1 = functools.partial(along_y, m1s, m1r, m1ss, m1sr, m1_send, m1_recv)
    m2 = functools.partial(along_y, m2s, m2r, m2ss, m2sr, m2_send, m2_recv)

    def across_x(t):
        return (
            remote(xs.at[t], xr.at[t], x_send.at[t, 0], x_recv.at[t, 0], to_x),
            remote(xss.at[t], xsr.at[t], x_send.at[t, 1], x_recv.at[t, 1], to_x),
        )

    def along_z(j, way, first=0, count=QUARTER):
        part_of = pl.ds(first, count)
        return (
            remote(zs.at[j, part_of], zr.at[j, part_of], z_send.at[j, 0], z_recv.at[j, 0], to_z(way)),
            remote(zss.at[j], zsr.at[j], z_send.at[j, 1], z_recv.at[j, 1], to_z(way)),
        )

    def start(copies):
        for copy in copies:
            copy.start()

    def wait_recv(copies):
        for copy in copies:
            copy.wait_recv()

    def wait_send(copies):
        for copy in copies:
            copy.wait_send()

    def multiply(t):
        for b in range(2):
            own_acts(t, b).wait()
        part[t] = jnp.dot(g_t[:, :TOK], a_own[t], preferred_element_type=F32)
        for b in range(2):
            pair_acts(t, b).wait_recv()
        part[t] += jnp.dot(g_t[:, TOK:], a_par[t], preferred_element_type=F32)
        up = jnp.concatenate([part[t, rows(2, 0, half_rows)], part[t, rows(1, half_rows, half_rows)]], axis=0)
        m1s[t, 0], m1ss[t, 0] = coded(up)
        start(m1(t, 0))
        down = jnp.concatenate([part[t, rows(2, half_rows, half_rows)], part[t, rows(3, 0, half_rows)]], axis=0)
        m1s[t, 1], m1ss[t, 1] = coded(down)
        start(m1(t, 1))

    def combine(t):
        wait_recv(m1(t, 0))
        got = plain(m1r[t, 0], m1sr[t, 0])
        m2s[t, 0], m2ss[t, 0] = coded(part[t, rows(1, 0, half_rows)] + got[A])
        start(m2(t, 0))
        part[t, rows(0, half_rows, half_rows)] += got[B]
        wait_recv(m1(t, 1))
        got = plain(m1r[t, 1], m1sr[t, 1])
        m2s[t, 1], m2ss[t, 1] = coded(part[t, rows(3, half_rows, half_rows)] + got[A])
        start(m2(t, 1))
        part[t, rows(0, 0, half_rows)] += got[B]

    def cross(t):
        wait_recv(m2(t, 0))
        part[t, rows(0, 0, half_rows)] += plain(m2r[t, 0], m2sr[t, 0])
        wait_recv(m2(t, 1))
        part[t, rows(0, half_rows, half_rows)] += plain(m2r[t, 1], m2sr[t, 1])
        xs[t], xss[t] = coded(part[t, rows(0), pl.ds(pl.multiple_of((1 - x) * HALF, HALF), HALF)])
        start(across_x(t))

    def crossed(t):
        wait_recv(across_x(t))
        return part[t, rows(0), pl.ds(pl.multiple_of(x * HALF, HALF), HALF)] + plain(xr[t], xsr[t])

    def travel(t):
        @pl.when(t == 0)
        def _():
            here = crossed(0)
            zs[0, A], zss[0] = coded(here[A])
            start(along_z(0, 1, 0, half_rows))
            zs[1, B], zss[1] = coded(here[B])
            start(along_z(1, -1, half_rows, half_rows))

        @pl.when(t == 1)
        def _():
            here = crossed(1)
            wait_recv(along_z(0, 1, 0, half_rows))
            zs[2], zss[2] = coded(jnp.concatenate([here[A] + plain(zr[0, A], zsr[0]), here[B]], axis=0))
            start(along_z(2, 1))

        @pl.when(t == 2)
        def _():
            here = crossed(2)
            wait_recv(along_z(1, -1, half_rows, half_rows))
            zs[3], zss[3] = coded(jnp.concatenate([here[A], here[B] + plain(zr[1, B], zsr[1])], axis=0))
            start(along_z(3, -1))

        for way in (1, -1):

            @pl.when((t >= 3) & (t <= 6) & (t % 2 == (1 if way == 1 else 0)))
            def _():
                here = crossed(t)
                wait_recv(along_z(t - 1, way))
                zs[t + 1], zss[t + 1] = coded(here + plain(zr[t - 1], zsr[t - 1]))
                start(along_z(t + 1, way))

        @pl.when(t == 7)
        def _():
            here = crossed(7)
            for way in (1, -1):
                j = 6 if way == 1 else 7
                wait_recv(along_z(j, way))
                here += plain(zr[j], zsr[j])
            fin[core * 4 + y], fin_scale[core * 4 + y] = coded(here)

    def weights(t):
        k = t // 2 + 1

        @pl.when(t == 0)
        def _():
            arrive(z, 1 - x, 0)
            for way in (1, -1):
                ring_copy(1, way, 0).start()
            pair_copy(z, 1 - x, 0).start()

        for flow, parity in ((0, 0), (2, 0), (1, 1)):
            for way in (1, -1):

                @pl.when((t % 2 == parity) & (k <= HOPS[way][flow]))
                def _():
                    ring_event(flow, way, k)

        @pl.when(t == 1)
        def _():
            x_event(1, 0)

        for way in (1, -1):

            @pl.when((t % 2 == 1) & (k >= 2))
            def _():
                x_event(way, k - 1)

    def step(t, carry):
        @pl.when(t < Z)
        def _():
            multiply(t)

        @pl.when((t >= 1) & (t <= Z))
        def _():
            weights(t - 1)

        @pl.when((t >= 2) & (t < Z + 2))
        def _():
            combine(t - 2)

        @pl.when((t >= 3) & (t < Z + 3))
        def _():
            cross(t - 3)

        @pl.when(t >= 4)
        def _():
            travel(t - 4)

        return carry

    lax.fori_loop(0, STEPS, step, 0)
    x_event(1, 4)

    def fin_copy(r, of, device, send, recv):
        at = of * 4 + ring(y - r, Y) if not isinstance(of, tuple) else of[0]
        return (
            remote(fin.at[at], fin.at[at], send.at[r, 0], recv.at[r, 0], device),
            remote(fin_scale.at[at], fin_scale.at[at], send.at[r, 1], recv.at[r, 1], device),
        )

    def to_replica(r):
        return fin_copy(r, (core * 4 + y,), to_y(r), f_send, f_recv)

    def to_partner(r):
        return fin_copy(r, core, to_pair, fp_send, fp_recv)

    for r in (2, 1, 3):
        start(to_replica(r))
    start(to_partner(0))
    for r in (1, 3, 2):
        wait_recv(fin_copy(r, core, to_y(r), f_send, f_recv))
        start(to_partner(r))
    for r in range(Y):
        wait_recv(fin_copy(r, 1 - core, to_pair, fp_send, fp_recv))

    own_cot.wait()
    pair_cot.wait_send()
    other = cot.at[:, pl.ds(pl.multiple_of((1 - tensor) * 256, 256), 256)]
    remote(pc, other, one.at[5], one.at[6], to_tensor).wait_recv()
    pair_g.wait_send()

    def finish(t, carry):
        for b in range(2):
            pair_acts(t, b).wait_send()
        for way in range(2):
            wait_send(m1(t, way))
            wait_send(m2(t, way))
        wait_send(across_x(t))
        return carry

    lax.fori_loop(0, Z, finish, 0)
    wait_send(along_z(0, 1, 0, half_rows))
    wait_send(along_z(1, -1, half_rows, half_rows))

    def finish_z(j, carry):
        wait_send(along_z(j, 1))
        return carry

    lax.fori_loop(2, Z, finish_z, 0)
    for r in range(Y):
        if r:
            wait_send(to_replica(r))
        wait_send(to_partner(r))
    for way in (1, -1):
        for flow in range(3):
            for k in range(HOPS[way][flow]):
                ring_copy(flow, way, k).wait_send()
    x_copy(z, 0, 0).wait_send()
    x_copy(z, 1, 1).wait_send()
    for way in (1, -1):
        for k in range(1, HOPS[way][2] + 1):
            x_copy(origin(way, k), 1, x_index(way, k)).wait_send()

    def finish_w(i, carry):
        zo, xo, half = i // 4, (i // 2) % 2, i % 2

        @pl.when(i // 2 != shard)
        def _():
            pair_copy(zo, xo, half).wait_send()
            at = w.at[slot(zo, xo, half, 1 - core)]
            remote(at, at, w_pair_send.at[i], w_pair_recv.at[i], to_pair).wait_recv()

        return carry

    lax.fori_loop(0, 4 * Z, finish_w, 0)


def gathered(acts, g, pv, pc):
    dma = pltpu.SemaphoreType.DMA
    any_, vmem = pl.BlockSpec(memory_space=pl.ANY), pl.BlockSpec(memory_space=pltpu.VMEM)
    S = jax.ShapeDtypeStruct
    return pl.pallas_call(
        exchange,
        out_shape=(S((64, 128, 512), BF16), S((256, 512), BF16), S((8, QUARTER, HALF), I16), S((8, 1, HALF), F32)),
        in_specs=[any_] * 4,
        out_specs=(vmem,) * 4,
        scratch_shapes=[
            pltpu.VMEM((Z, TOK, 2 * HALF), BF16),
            pltpu.VMEM((Z, TOK, 2 * HALF), BF16),
            pltpu.VMEM((2, TOK, COLS), BF16),
            pltpu.VMEM((COLS, 2 * TOK), BF16),
            pltpu.VMEM((Z, COLS, 2 * HALF), F32),
            *[pltpu.VMEM((Z, 2, QUARTER, 2 * HALF), I16)] * 2,
            *[pltpu.VMEM((Z, 2, 1, 2 * HALF), F32)] * 2,
            *[pltpu.VMEM((Z, 2, QUARTER // 2, 2 * HALF), I16)] * 2,
            *[pltpu.VMEM((Z, 2, 1, 2 * HALF), F32)] * 2,
            *[pltpu.VMEM((Z, QUARTER, HALF), I16)] * 2,
            *[pltpu.VMEM((Z, 1, HALF), F32)] * 2,
            *[pltpu.VMEM((Z, QUARTER, HALF), I16)] * 2,
            *[pltpu.VMEM((Z, 1, HALF), F32)] * 2,
            dma((Z, 2)), dma((Z, 2)), dma((Z, 2)), dma((7,)),
            dma((32,)), dma((32,)), dma((2, 12)), dma((10,)), dma((32,)),
            dma((Z, 2, 2)), dma((Z, 2, 2)), dma((Z, 2, 2)), dma((Z, 2, 2)),
            dma((Z, 2)), dma((Z, 2)), dma((Z, 2)), dma((Z, 2)),
            dma((Y, 2)), dma((Y, 2)), dma((Y, 2)), dma((Y, 2)),
        ],
        compiler_params=pltpu.CompilerParams(
            collective_id=1, has_side_effects=True, vmem_limit_bytes=48 << 20
        ),
    )(acts, g, pv.reshape(4, 128, 512), pc)


def local(
    activations,
    value_cotangent,
    key_gradient,
    key_master,
    key_moment,
    key_second,
    step_count,
    previous_value,
    previous_cotangent,
):
    weights, cotangent, fin, fin_scale = gathered(activations, value_cotangent, previous_value, previous_cotangent)
    blocks = (fin.astype(F32) * fin_scale).reshape(2, Y, QUARTER, HALF)
    value_grad = blocks.transpose(0, 3, 1, 2).reshape(2 * HALF, COLS)
    moment_new = 0.9 * key_moment + 0.1 * key_gradient
    second_new = 0.95 * key_second + 0.05 * key_gradient * key_gradient
    steps_done = step_count.astype(jnp.float32)[0]
    first_fix = 1.0 - jnp.power(jnp.float32(0.9), steps_done)
    second_fix = 1.0 - jnp.power(jnp.float32(0.95), steps_done)
    key_update = (
        moment_new / first_fix / (jnp.sqrt(second_new / second_fix) + 1e-08) + 0.1 * key_master
    )
    input_grad = lax.dot_general(
        cotangent,
        weights.reshape(FEAT, COLS),
        (((1,), (1,)), ((), ())),
        preferred_element_type=jnp.float32,
    ).astype(jnp.bfloat16)
    return (value_grad, moment_new, second_new, key_update, input_grad)


def solution(mesh):
    in_specs = (
        P(("shard", "replica"), "tensor"),
        P(("shard", "replica"), None),
        P("shard", "tensor"),
        P("shard", "tensor"),
        P("shard", "tensor"),
        P("shard", "tensor"),
        P(),
        P(("tensor", "shard"), None),
        P(("shard", "replica"), "tensor"),
    )
    out_specs = (
        P(("tensor", "shard"), None),
        P("shard", "tensor"),
        P("shard", "tensor"),
        P("shard", "tensor"),
        P(("shard", "replica"), "tensor"),
    )
    return jax.shard_map(local, mesh=mesh, in_specs=in_specs, out_specs=out_specs, check_vma=False)
```

```python
import functools
import math

import jax
import jax.numpy as jnp
from jax import lax
from jax.experimental import pallas as pl
from jax.experimental.pallas import tpu as pltpu
from jax.sharding import PartitionSpec as P

MESH = pl.DeviceIdType.MESH
F32, BF16, I16, I32 = jnp.float32, jnp.bfloat16, jnp.int16, jnp.int32
Z, Y = 8, 4
TOK, FEAT, COLS = 256, 8192, 512
HALF = 256
QUARTER = COLS // Y
AHEAD = 3
CROSS_LAG, TRAVEL_LAG = 3, 5
SPLIT = 160
LOG_KEEP_FIRST, LOG_KEEP_SECOND = math.log(0.9), math.log(0.95)
HOPS = {1: (4, 3, 4), -1: (3, 4, 3)}


def coded(x):
    top = jnp.maximum(jnp.max(jnp.abs(x), axis=0, keepdims=True), 1e-30)
    return jnp.round(x * (32767.0 / top)).astype(I32).astype(I16), top * (1.0 / 32767.0)


def plain(q, scale):
    return q.astype(I32).astype(F32) * scale


def exchange(
    steps, acts, g, pv, pc, key_in,
    input_grad, key_out, fin, fin_scale,
    w, cot, key_buf, a_own, a_par, g_buf, g_t, part,
    m1s, m1r, m1ss, m1sr, m2s, m2r, m2ss, m2sr,
    xs, xr, xss, xsr, zs, zr, zss, zsr,
    key_sem, a_local, a_send, a_recv, one, w_recv, w_pair_recv, w_ring_send, w_x_send, w_pair_send,
    m1_send, m1_recv, m2_send, m2_recv, x_send, x_recv, z_send, z_recv, f_send, f_recv, fp_send, fp_recv,
):
    tensor = lax.axis_index("tensor")
    shard = lax.axis_index("shard")
    replica = lax.axis_index("replica")
    z, x = shard // 2, shard % 2
    y, core = replica // 2, replica % 2
    sgn = 1 - 2 * core

    def ring(at, n):
        return lax.rem(at + 2 * n, n)

    to_pair = (tensor, shard, y * 2 + 1 - core)
    to_x = (tensor, z * 2 + 1 - x, replica)
    to_tensor = (1 - tensor, shard, replica)

    def to_y(r):
        return (tensor, shard, ring(y + r, Y) * 2 + core)

    def to_z(way):
        return (tensor, ring(z + way * sgn, Z) * 2 + x, replica)

    def remote(src, dst, send, recv, device):
        return pltpu.make_async_remote_copy(
            src_ref=src, dst_ref=dst, send_sem=send, recv_sem=recv, device_id=device, device_id_type=MESH
        )

    barrier = pltpu.get_barrier_semaphore()
    peers = (to_pair, to_x, to_tensor, to_y(1), to_y(2), to_y(3), to_z(1), to_z(-1))
    for peer in peers:
        pl.semaphore_signal(barrier, inc=1, device_id=peer, device_id_type=MESH)

    def columns(t, b, of_core):
        far = Z // 2 - (t + 1) // 2
        offset = jnp.where(t % 2 == 1, far, -far) * (1 - 2 * of_core)
        start = (ring(z + offset, Z) * 2 + b) * 2 * HALF + of_core * HALF
        return pl.ds(pl.multiple_of(start, HALF), HALF)

    def own_acts(t, b):
        return pltpu.make_async_copy(
            acts.at[:, columns(t, b, core)], a_own.at[t, :, pl.ds(b * HALF, HALF)], a_local.at[t, b]
        )

    def pair_acts(t, b):
        return remote(
            acts.at[:, columns(t, b, 1 - core)], a_par.at[t, :, pl.ds(b * HALF, HALF)],
            a_send.at[t, b], a_recv.at[t, b], to_pair,
        )

    own_g = pltpu.make_async_copy(g, g_buf.at[0], one.at[0])
    pair_g = remote(g, g_buf.at[1], one.at[1], one.at[2], to_pair)
    own_w = pltpu.make_async_copy(pv, w.at[shard], one.at[3])
    own_cot = pltpu.make_async_copy(pc, cot.at[:, pl.ds(pl.multiple_of(tensor * 256, 256), 256)], one.at[4])
    pair_cot = remote(pc, cot.at[:, pl.ds(pl.multiple_of(tensor * 256, 256), 256)], one.at[5], one.at[6], to_tensor)

    def block(zo, xo, half, of_core):
        first, count = ((0, SPLIT), (SPLIT, HALF - SPLIT))[half]
        return w.at[zo * 2 + xo, pl.ds(pl.multiple_of(of_core * HALF + first, 16), count)]

    def mark(zo, xo, half):
        return (zo * 2 + xo) * 2 + half

    def flow_of(flow):
        return (1 - x if flow == 1 else x), (1 if flow == 2 else 0)

    def origin(way, k):
        return ring(z - way * sgn * k, Z)

    def ring_copy(flow, way, k):
        xo, half = flow_of(flow)
        zo = origin(way, k)
        at = block(zo, xo, half, core)
        return remote(at, at, w_ring_send.at[0 if way == 1 else 1, flow * 4 + k], w_recv.at[mark(zo, xo, half)], to_z(way))

    def x_copy(zo, half, k):
        at = block(zo, x, half, core)
        return remote(at, at, w_x_send.at[k], w_recv.at[mark(zo, x, half)], to_x)

    def pair_copy(zo, xo, half):
        at = block(zo, xo, half, core)
        return remote(at, at, w_pair_send.at[mark(zo, xo, half)], w_pair_recv.at[mark(zo, xo, half)], to_pair)

    def arrive(zo, xo, half):
        at = block(zo, xo, half, core)
        remote(at, at, w_x_send.at[0], w_recv.at[mark(zo, xo, half)], to_x).wait_recv()

    def x_index(way, k):
        return 2 * k + (0 if way == 1 else 1)

    def ring_event(flow, way, k):
        xo, half = flow_of(flow)
        zo = origin(way, k)
        arrive(zo, xo, half)

        @pl.when(k < HOPS[way][flow])
        def _():
            ring_copy(flow, way, k).start()

        if flow == 2:
            x_copy(zo, half, x_index(way, k)).start()
        pair_copy(zo, xo, half).start()

    def x_event(way, k):
        zo = origin(way, k)
        arrive(zo, 1 - x, 1)
        pair_copy(zo, 1 - x, 1).start()

    def key_copy(i):
        return pltpu.make_async_copy(key_in[i], key_buf.at[i], key_sem.at[i])

    def turned_g(b):
        for r in range(Y):
            take = pl.ds(pl.multiple_of(ring(y + r, Y) * QUARTER, QUARTER), QUARTER)
            g_t[r * QUARTER : (r + 1) * QUARTER, b * TOK : (b + 1) * TOK] = (
                g_buf[b, :, take].astype(F32).T.astype(BF16)
            )

    def start_own(t, carry):
        for b in range(2):
            own_acts(t, b).start()
        return carry

    def start_pair(t, carry):
        for b in range(2):
            pair_acts(t, b).start()
        return carry

    own_g.start()
    own_w.start()
    lax.fori_loop(0, Z, start_own, 0)
    own_cot.start()
    for i in range(4):
        key_copy(i).start()
    own_g.wait()
    turned_g(0)
    own_w.wait()
    pl.semaphore_wait(barrier, len(peers))

    pair_g.start()
    lax.fori_loop(0, 1, start_pair, 0)
    pair_cot.start()
    x_copy(z, 0, 0).start()
    for way in (1, -1):
        ring_copy(0, way, 0).start()
    x_copy(z, 1, 1).start()
    for way in (1, -1):
        ring_copy(2, way, 0).start()
    lax.fori_loop(1, Z, start_pair, 0)
    pair_g.wait_recv()
    turned_g(1)

    A, B = slice(0, QUARTER // 2), slice(QUARTER // 2, QUARTER)
    half_rows = QUARTER // 2

    def rows(r, first=0, count=QUARTER):
        return pl.ds(r * QUARTER + first, count)

    def along_y(src, dst, src_scale, dst_scale, send, recv, t, way):
        to = to_y(1 if way == 0 else 3)
        return (
            remote(src.at[t, way], dst.at[t, way], send.at[t, way, 0], recv.at[t, way, 0], to),
            remote(src_scale.at[t, way], dst_scale.at[t, way], send.at[t, way, 1], recv.at[t, way, 1], to),
        )

    m1 = functools.partial(along_y, m1s, m1r, m1ss, m1sr, m1_send, m1_recv)
    m2 = functools.partial(along_y, m2s, m2r, m2ss, m2sr, m2_send, m2_recv)

    def across_x(t):
        return (
            remote(xs.at[t], xr.at[t], x_send.at[t, 0], x_recv.at[t, 0], to_x),
            remote(xss.at[t], xsr.at[t], x_send.at[t, 1], x_recv.at[t, 1], to_x),
        )

    def along_z(j, way, first=0, count=QUARTER):
        part_of = pl.ds(first, count)
        return (
            remote(zs.at[j, part_of], zr.at[j, part_of], z_send.at[j, 0], z_recv.at[j, 0], to_z(way)),
            remote(zss.at[j], zsr.at[j], z_send.at[j, 1], z_recv.at[j, 1], to_z(way)),
        )

    def start(copies):
        for copy in copies:
            copy.start()

    def wait_recv(copies):
        for copy in copies:
            copy.wait_recv()

    def wait_send(copies):
        for copy in copies:
            copy.wait_send()

    def multiply(t):
        for b in range(2):
            own_acts(t, b).wait()
        part[t] = jnp.dot(g_t[:, :TOK], a_own[t], preferred_element_type=F32)
        for b in range(2):
            pair_acts(t, b).wait_recv()
        part[t] += jnp.dot(g_t[:, TOK:], a_par[t], preferred_element_type=F32)
        up = jnp.concatenate([part[t, rows(2, 0, half_rows)], part[t, rows(1, half_rows, half_rows)]], axis=0)
        m1s[t, 0], m1ss[t, 0] = coded(up)
        start(m1(t, 0))
        down = jnp.concatenate([part[t, rows(2, half_rows, half_rows)], part[t, rows(3, 0, half_rows)]], axis=0)
        m1s[t, 1], m1ss[t, 1] = coded(down)
        start(m1(t, 1))

    def combine(t):
        wait_recv(m1(t, 0))
        got = plain(m1r[t, 0], m1sr[t, 0])
        m2s[t, 0], m2ss[t, 0] = coded(part[t, rows(1, 0, half_rows)] + got[A])
        start(m2(t, 0))
        part[t, rows(0, half_rows, half_rows)] += got[B]
        wait_recv(m1(t, 1))
        got = plain(m1r[t, 1], m1sr[t, 1])
        m2s[t, 1], m2ss[t, 1] = coded(part[t, rows(3, half_rows, half_rows)] + got[A])
        start(m2(t, 1))
        part[t, rows(0, 0, half_rows)] += got[B]

    def cross(t):
        wait_recv(m2(t, 0))
        part[t, rows(0, 0, half_rows)] += plain(m2r[t, 0], m2sr[t, 0])
        wait_recv(m2(t, 1))
        part[t, rows(0, half_rows, half_rows)] += plain(m2r[t, 1], m2sr[t, 1])
        xs[t], xss[t] = coded(part[t, rows(0), pl.ds(pl.multiple_of((1 - x) * HALF, HALF), HALF)])
        start(across_x(t))

    def crossed(t):
        wait_recv(across_x(t))
        return part[t, rows(0), pl.ds(pl.multiple_of(x * HALF, HALF), HALF)] + plain(xr[t], xsr[t])

    def travel(t):
        @pl.when(t == 0)
        def _():
            here = crossed(0)
            zs[0, A], zss[0] = coded(here[A])
            start(along_z(0, 1, 0, half_rows))
            zs[1, B], zss[1] = coded(here[B])
            start(along_z(1, -1, half_rows, half_rows))

        @pl.when(t == 1)
        def _():
            here = crossed(1)
            wait_recv(along_z(0, 1, 0, half_rows))
            zs[2], zss[2] = coded(jnp.concatenate([here[A] + plain(zr[0, A], zsr[0]), here[B]], axis=0))
            start(along_z(2, 1))

        @pl.when(t == 2)
        def _():
            here = crossed(2)
            wait_recv(along_z(1, -1, half_rows, half_rows))
            zs[3], zss[3] = coded(jnp.concatenate([here[A], here[B] + plain(zr[1, B], zsr[1])], axis=0))
            start(along_z(3, -1))

        for way in (1, -1):

            @pl.when((t >= 3) & (t <= 6) & (t % 2 == (1 if way == 1 else 0)))
            def _():
                here = crossed(t)
                wait_recv(along_z(t - 1, way))
                zs[t + 1], zss[t + 1] = coded(here + plain(zr[t - 1], zsr[t - 1]))
                start(along_z(t + 1, way))

        @pl.when(t == 7)
        def _():
            here = crossed(7)
            for way in (1, -1):
                j = 6 if way == 1 else 7
                wait_recv(along_z(j, way))
                here += plain(zr[j], zsr[j])
            fin[core * 4 + y], fin_scale[core * 4 + y] = coded(here)

    def weights(i):
        for flow, k, now in ((0, i // 2 + 1, i % 2 == 0), (1, i // 2, (i % 2 == 0) & (i > 0)), (2, (i + 1) // 2, i % 2 == 1)):
            for way in (1, -1):

                @pl.when(now & (k <= HOPS[way][flow]))
                def _():
                    ring_event(flow, way, k)

    def weights_across(i):
        @pl.when(i == 1)
        def _():
            x_event(1, 0)

        for way in (1, -1):

            @pl.when((i % 2 == 1) & (i >= 3) & (i <= 7))
            def _():
                x_event(way, (i - 1) // 2)

    def adam(t):
        at = pl.ds(pl.multiple_of(t * QUARTER, QUARTER), QUARTER)
        gradient, master, moment, second = (key_buf[i, at] for i in range(4))
        count = jnp.full((1, HALF), steps[0], I32).astype(F32)
        moment_new = 0.9 * moment + 0.1 * gradient
        second_new = 0.95 * second + 0.05 * gradient * gradient
        first_fix = 1.0 - jnp.exp(count * LOG_KEEP_FIRST)
        second_fix = 1.0 - jnp.exp(count * LOG_KEEP_SECOND)
        key_out[0, at] = moment_new
        key_out[1, at] = second_new
        key_out[2, at] = moment_new / first_fix / (jnp.sqrt(second_new / second_fix) + 1e-08) + 0.1 * master

    def product(i):
        zo = ring(z + jnp.where(i % 2 == 1, (i + 1) // 2, -(i // 2)), Z)
        for xo in range(2):

            @pl.when(zo * 2 + xo != shard)
            def _():
                for half in range(2):
                    at = block(zo, xo, half, 1 - core)
                    remote(at, at, w_pair_send.at[0], w_pair_recv.at[mark(zo, xo, half)], to_pair).wait_recv()

            to = pl.ds(pl.multiple_of((zo * 2 + xo) * 2 * HALF, 2 * HALF), 2 * HALF)
            input_grad[:, to] = lax.dot_general(
                cot[...], w[zo * 2 + xo], (((1,), (1,)), ((), ())), preferred_element_type=F32
            ).astype(BF16)

    def first(t, carry):
        multiply(t)
        return carry

    def step(i, carry):
        @pl.when(i < Z)
        def _():
            combine(i)

        @pl.when(i + AHEAD < Z)
        def _():
            multiply(i + AHEAD)

        @pl.when(i <= Z)
        def _():
            weights(i)

        @pl.when((i >= CROSS_LAG) & (i < CROSS_LAG + Z))
        def _():
            cross(i - CROSS_LAG)

        @pl.when(i >= TRAVEL_LAG)
        def _():
            travel(i - TRAVEL_LAG)

        @pl.when(i < Z)
        def _():
            weights_across(i)
            adam(i)

        @pl.when((i >= 4) & (i < 7))
        def _():
            product(i - 4)

        @pl.when((i >= 8) & (i < 10))
        def _():
            product(i - 5)

        return carry

    lax.fori_loop(0, AHEAD, first, 0)
    arrive(z, 1 - x, 0)
    for way in (1, -1):
        ring_copy(1, way, 0).start()
    pair_copy(z, 1 - x, 0).start()
    for i in range(4):
        key_copy(i).wait()
    own_cot.wait()
    other = cot.at[:, pl.ds(pl.multiple_of((1 - tensor) * 256, 256), 256)]
    remote(pc, other, one.at[5], one.at[6], to_tensor).wait_recv()
    lax.fori_loop(0, TRAVEL_LAG + Z, step, 0)
    x_event(1, 4)

    def fin_copy(r, of, device, send, recv):
        at = of * 4 + ring(y - r, Y) if not isinstance(of, tuple) else of[0]
        return (
            remote(fin.at[at], fin.at[at], send.at[r, 0], recv.at[r, 0], device),
            remote(fin_scale.at[at], fin_scale.at[at], send.at[r, 1], recv.at[r, 1], device),
        )

    def to_replica(r):
        return fin_copy(r, (core * 4 + y,), to_y(r), f_send, f_recv)

    def to_partner(r):
        return fin_copy(r, core, to_pair, fp_send, fp_recv)

    for r in (2, 1, 3):
        start(to_replica(r))
    start(to_partner(0))
    def products(i, carry):
        product(i)
        return carry

    lax.fori_loop(5, Z, products, 0)
    for r in (1, 3, 2):
        wait_recv(fin_copy(r, core, to_y(r), f_send, f_recv))
        start(to_partner(r))
    for r in range(Y):
        wait_recv(fin_copy(r, 1 - core, to_pair, fp_send, fp_recv))

    pair_cot.wait_send()
    pair_g.wait_send()

    def finish(t, carry):
        for b in range(2):
            pair_acts(t, b).wait_send()
        for way in range(2):
            wait_send(m1(t, way))
            wait_send(m2(t, way))
        wait_send(across_x(t))
        return carry

    lax.fori_loop(0, Z, finish, 0)
    wait_send(along_z(0, 1, 0, half_rows))
    wait_send(along_z(1, -1, half_rows, half_rows))

    def finish_z(j, carry):
        wait_send(along_z(j, 1))
        return carry

    lax.fori_loop(2, Z, finish_z, 0)
    for r in range(Y):
        if r:
            wait_send(to_replica(r))
        wait_send(to_partner(r))
    for way in (1, -1):
        for flow in range(3):
            for k in range(HOPS[way][flow]):
                ring_copy(flow, way, k).wait_send()
    x_copy(z, 0, 0).wait_send()
    x_copy(z, 1, 1).wait_send()
    for way in (1, -1):
        for k in range(1, HOPS[way][2] + 1):
            x_copy(origin(way, k), 1, x_index(way, k)).wait_send()

    def finish_w(i, carry):
        @pl.when(i != shard)
        def _():
            for half in range(2):
                pair_copy(i // 2, i % 2, half).wait_send()

        return carry

    lax.fori_loop(0, 2 * Z, finish_w, 0)


def gathered(steps, acts, g, pv, pc, keys):
    dma = pltpu.SemaphoreType.DMA
    hbm, vmem = pl.BlockSpec(memory_space=pltpu.HBM), pl.BlockSpec(memory_space=pltpu.VMEM)
    in_hbm = [pltpu.with_memory_space_constraint(v, pltpu.HBM) for v in (acts, g, pv, pc, *keys)]

    def body(steps, acts, g, pv, pc, k0, k1, k2, k3, *rest):
        exchange(steps, acts, g, pv, pc, (k0, k1, k2, k3), *rest)

    return pl.pallas_call(
        body,
        out_shape=(
            pltpu.VMEM((TOK, FEAT), BF16),
            pltpu.VMEM((3, 1024, 256), F32),
            pltpu.VMEM((8, QUARTER, HALF), I16),
            pltpu.VMEM((8, 1, HALF), F32),
        ),
        in_specs=[pl.BlockSpec(memory_space=pltpu.SMEM)] + [hbm] * 8,
        out_specs=(vmem,) * 4,
        scratch_shapes=[
            pltpu.VMEM((2 * Z, 2 * HALF, COLS), BF16),
            pltpu.VMEM((TOK, COLS), BF16),
            pltpu.VMEM((4, 1024, 256), F32),
            pltpu.VMEM((Z, TOK, 2 * HALF), BF16),
            pltpu.VMEM((Z, TOK, 2 * HALF), BF16),
            pltpu.VMEM((2, TOK, COLS), BF16),
            pltpu.VMEM((COLS, 2 * TOK), BF16),
            pltpu.VMEM((Z, COLS, 2 * HALF), F32),
            *[pltpu.VMEM((Z, 2, QUARTER, 2 * HALF), I16)] * 2,
            *[pltpu.VMEM((Z, 2, 1, 2 * HALF), F32)] * 2,
            *[pltpu.VMEM((Z, 2, QUARTER // 2, 2 * HALF), I16)] * 2,
            *[pltpu.VMEM((Z, 2, 1, 2 * HALF), F32)] * 2,
            *[pltpu.VMEM((Z, QUARTER, HALF), I16)] * 2,
            *[pltpu.VMEM((Z, 1, HALF), F32)] * 2,
            *[pltpu.VMEM((Z, QUARTER, HALF), I16)] * 2,
            *[pltpu.VMEM((Z, 1, HALF), F32)] * 2,
            dma((4,)), dma((Z, 2)), dma((Z, 2)), dma((Z, 2)), dma((7,)),
            dma((32,)), dma((32,)), dma((2, 12)), dma((10,)), dma((32,)),
            dma((Z, 2, 2)), dma((Z, 2, 2)), dma((Z, 2, 2)), dma((Z, 2, 2)),
            dma((Z, 2)), dma((Z, 2)), dma((Z, 2)), dma((Z, 2)),
            dma((Y, 2)), dma((Y, 2)), dma((Y, 2)), dma((Y, 2)),
        ],
        compiler_params=pltpu.CompilerParams(
            collective_id=1, has_side_effects=True, vmem_limit_bytes=44 << 20
        ),
    )(steps, *in_hbm)


def write_out(input_grad, key_out, fin, fin_scale, value_to, moment_to, second_to, update_to, input_to, value_grad, sems):
    copies = [
        pltpu.make_async_copy(input_grad.at[pl.ds(i * 64, 64)], input_to.at[pl.ds(i * 64, 64)], sems.at[i])
        for i in range(4)
    ]
    for i, to in enumerate((moment_to, second_to, update_to)):
        copies.append(pltpu.make_async_copy(key_out.at[i], to, sems.at[4 + i]))
    for copy in copies:
        copy.start()
    for core in range(2):
        for y in range(Y):
            value_grad[core * HALF : (core + 1) * HALF, y * QUARTER : (y + 1) * QUARTER] = plain(
                fin[core * 4 + y], fin_scale[core * 4 + y]
            ).T
    last = pltpu.make_async_copy(value_grad, value_to, sems.at[7])
    last.start()
    for copy in copies:
        copy.wait()
    last.wait()


def written(arrays):
    S = jax.ShapeDtypeStruct
    key = S((1024, 256), F32)
    return pl.pallas_call(
        write_out,
        out_shape=(S((2 * HALF, COLS), F32), key, key, key, S((TOK, FEAT), BF16)),
        in_specs=[pl.BlockSpec(memory_space=pltpu.VMEM)] * 4,
        out_specs=(pl.BlockSpec(memory_space=pltpu.HBM),) * 5,
        scratch_shapes=[pltpu.VMEM((2 * HALF, COLS), F32), pltpu.SemaphoreType.DMA((8,))],
        compiler_params=pltpu.CompilerParams(vmem_limit_bytes=8 << 20),
    )(*[pltpu.with_memory_space_constraint(v, pltpu.VMEM) for v in arrays])


def local(
    activations,
    value_cotangent,
    key_gradient,
    key_master,
    key_moment,
    key_second,
    step_count,
    previous_value,
    previous_cotangent,
):
    keys = (key_gradient, key_master, key_moment, key_second)
    return tuple(written(gathered(
        step_count, activations, value_cotangent, previous_value, previous_cotangent, keys
    )))


def solution(mesh):
    in_specs = (
        P(("shard", "replica"), "tensor"),
        P(("shard", "replica"), None),
        P("shard", "tensor"),
        P("shard", "tensor"),
        P("shard", "tensor"),
        P("shard", "tensor"),
        P(),
        P(("tensor", "shard"), None),
        P(("shard", "replica"), "tensor"),
    )
    out_specs = (
        P(("tensor", "shard"), None),
        P("shard", "tensor"),
        P("shard", "tensor"),
        P("shard", "tensor"),
        P(("shard", "replica"), "tensor"),
    )
    return jax.shard_map(local, mesh=mesh, in_specs=in_specs, out_specs=out_specs, check_vma=False)
```

```python
import functools
import math

import jax
import jax.numpy as jnp
from jax import lax
from jax.experimental import pallas as pl
from jax.experimental.pallas import tpu as pltpu
from jax.sharding import PartitionSpec as P

MESH = pl.DeviceIdType.MESH
F32, BF16, I16, I32 = jnp.float32, jnp.bfloat16, jnp.int16, jnp.int32
Z, Y = 8, 4
TOK, FEAT, COLS = 256, 8192, 512
HALF = 256
QUARTER = COLS // Y
AHEAD = 3
CROSS_LAG, TRAVEL_LAG, WEIGHT_LAG = 2, 4, 1
SPLIT = 160
PARTS = ((0, SPLIT), (SPLIT, HALF - SPLIT))
ACROSS = 12
LOG_KEEP_FIRST, LOG_KEEP_SECOND = math.log(0.9), math.log(0.95)
HOPS = {1: (4, 3, 4), -1: (3, 4, 3)}


def coded(x):
    top = jnp.maximum(jnp.max(jnp.abs(x), axis=0, keepdims=True), 1e-30)
    return jnp.round(x * (32767.0 / top)).astype(I32).astype(I16), top * (1.0 / 32767.0)


def plain(q, scale):
    return q.astype(I32).astype(F32) * scale


def exchange(
    steps, acts, g, pv, pc, key_in,
    input_grad, key_out, fin, fin_scale,
    w, cot, key_buf, a_own, a_par, g_buf, g_t, part,
    m1s, m1r, m1ss, m1sr, m2s, m2r, m2ss, m2sr,
    xs, xr, xss, xsr, zs, zr, zss, zsr, tally,
    one, a_recv, w_recv, w_pair_recv, sent, m1_recv, m2_recv, x_recv, z_recv, f_recv,
):
    tensor = lax.axis_index("tensor")
    shard = lax.axis_index("shard")
    replica = lax.axis_index("replica")
    z, x = shard // 2, shard % 2
    y, core = replica // 2, replica % 2
    sgn = 1 - 2 * core

    def ring(at, n):
        return lax.rem(at + 2 * n, n)

    to_pair = (tensor, shard, y * 2 + 1 - core)
    to_x = (tensor, z * 2 + 1 - x, replica)
    to_tensor = (1 - tensor, shard, replica)

    def to_y(r):
        return (tensor, shard, ring(y + r, Y) * 2 + core)

    def to_z(way):
        return (tensor, ring(z + way * sgn, Z) * 2 + x, replica)

    def remote(src, dst, send, recv, device):
        return pltpu.make_async_remote_copy(
            src_ref=src, dst_ref=dst, send_sem=send, recv_sem=recv, device_id=device, device_id_type=MESH
        )

    def await_bytes(sem, *refs):
        for ref in refs:
            pltpu.make_async_copy(ref, ref, sem).wait()

    def units(n):
        return tally.at[pl.ds(0, n)]

    barrier = pltpu.get_barrier_semaphore()
    peers = (to_pair, to_x, to_tensor, to_y(1), to_y(2), to_y(3), to_z(1), to_z(-1))
    for peer in peers:
        pl.semaphore_signal(barrier, inc=1, device_id=peer, device_id_type=MESH)

    def columns(t, b, of_core):
        far = Z // 2 - (t + 1) // 2
        offset = jnp.where(t % 2 == 1, far, -far) * (1 - 2 * of_core)
        start = (ring(z + offset, Z) * 2 + b) * 2 * HALF + of_core * HALF
        return pl.ds(pl.multiple_of(start, HALF), HALF)

    def start_own(t, carry):
        for b in range(2):
            to = a_own.at[t, :, pl.ds(b * HALF, HALF)]
            pltpu.make_async_copy(acts.at[:, columns(t, b, core)], to, one.at[0]).start()
        return carry

    def start_pair(t, carry):
        for b in range(2):
            to = a_par.at[t, :, pl.ds(b * HALF, HALF)]
            remote(acts.at[:, columns(t, b, 1 - core)], to, sent.at[0], a_recv.at[t], to_pair).start()
        return carry

    own_g = pltpu.make_async_copy(g, g_buf.at[0], one.at[1])
    pair_g = remote(g, g_buf.at[1], one.at[2], one.at[3], to_pair)
    own_w = pltpu.make_async_copy(pv, w.at[pl.ds(pl.multiple_of(shard * 2 * HALF, 2 * HALF), 2 * HALF)], one.at[4])
    cot_at = cot.at[:, pl.ds(pl.multiple_of(tensor * 256, 256), 256)]
    own_cot = pltpu.make_async_copy(pc, cot_at, one.at[5])
    pair_cot = remote(pc, cot_at, one.at[6], one.at[7], to_tensor)

    def block(zo, xo, half):
        first, count = PARTS[half]
        return w.at[pl.ds(pl.multiple_of((zo * 2 + xo) * 2 * HALF + core * HALF + first, 16), count)]

    def own_block(half):
        first, count = PARTS[half]
        return pv.at[pl.ds(pl.multiple_of(core * HALF + first, 16), count)]

    def flow_of(flow):
        return (1 - x if flow == 1 else x), (1 if flow == 2 else 0)

    def origin(way, k):
        return ring(z - way * sgn * k, Z)

    def ring_send(flow, way, k, source=None):
        xo, half = flow_of(flow)
        at = block(origin(way, k), xo, half)
        remote(at if source is None else source, at, sent.at[1], w_recv.at[flow * 4 + k], to_z(way)).start()

    def x_send(zo, half, mark, source=None):
        at = block(zo, x, half)
        remote(at if source is None else source, at, sent.at[2], w_recv.at[mark], to_x).start()

    def pair_send(zo, xo, half):
        at = block(zo, xo, half)
        remote(at, at, sent.at[3], w_pair_recv.at[zo], to_pair).start()

    def arrive(mark, half, count):
        await_bytes(w_recv.at[mark], w.at[pl.ds(0, count * PARTS[half][1])])

    def ring_events(flow, k, ways):
        xo, half = flow_of(flow)
        arrive(flow * 4 + k - 1, half, len(ways))
        for way in ways:

            @pl.when(k < HOPS[way][flow])
            def _():
                ring_send(flow, way, k)

        for way in ways:
            zo = origin(way, k)
            if flow == 2:
                x_send(zo, half, ACROSS + 1 + k)
            pair_send(zo, xo, half)

    def x_events(k, ways):
        arrive(ACROSS + 1 + k, 1, len(ways))
        for way in ways:
            pair_send(origin(way, k), 1 - x, 1)

    def turned_g(b):
        for r in range(Y):
            take = pl.ds(pl.multiple_of(ring(y + r, Y) * QUARTER, QUARTER), QUARTER)
            g_t[r * QUARTER : (r + 1) * QUARTER, b * TOK : (b + 1) * TOK] = (
                g_buf[b, :, take].astype(F32).T.astype(BF16)
            )

    own_g.start()
    lax.fori_loop(0, Z, start_own, 0)
    pl.semaphore_wait(barrier, len(peers))
    pair_g.start()
    lax.fori_loop(0, 1, start_pair, 0)
    x_send(z, 0, ACROSS, own_block(0))
    for way in (1, -1):
        ring_send(0, way, 0, own_block(0))
    pair_cot.start()
    x_send(z, 1, ACROSS + 1, own_block(1))
    for way in (1, -1):
        ring_send(2, way, 0, own_block(1))
    lax.fori_loop(1, Z, start_pair, 0)
    own_w.start()
    own_cot.start()
    for i in range(4):
        pltpu.make_async_copy(key_in[i], key_buf.at[i], one.at[8]).start()
    own_g.wait()
    turned_g(0)
    await_bytes(one.at[0], a_own)

    A, B = slice(0, QUARTER // 2), slice(QUARTER // 2, QUARTER)
    half_rows = QUARTER // 2

    def rows(r, first=0, count=QUARTER):
        return pl.ds(r * QUARTER + first, count)

    def send_y(src, dst, src_scale, dst_scale, send, recv, t):
        for way in range(2):
            to = to_y(1 if way == 0 else 3)
            remote(src.at[t, way], dst.at[t, way], sent.at[send], recv.at[t], to).start()
            remote(src_scale.at[t, way], dst_scale.at[t, way], sent.at[send + 1], recv.at[t], to).start()

    def send_z(j, way, first=0, count=QUARTER):
        some = pl.ds(first, count)
        remote(zs.at[j, some], zr.at[j, some], sent.at[10], z_recv.at[j], to_z(way)).start()
        remote(zss.at[j], zsr.at[j], sent.at[11], z_recv.at[j], to_z(way)).start()

    def multiply_own(t):
        part[t] = jnp.dot(g_t[:, :TOK], a_own[t], preferred_element_type=F32)

    def multiply(t):
        await_bytes(a_recv.at[t], a_par.at[t])
        part[t] += jnp.dot(g_t[:, TOK:], a_par[t], preferred_element_type=F32)
        up = jnp.concatenate([part[t, rows(2, 0, half_rows)], part[t, rows(1, half_rows, half_rows)]], axis=0)
        m1s[t, 0], m1ss[t, 0] = coded(up)
        down = jnp.concatenate([part[t, rows(2, half_rows, half_rows)], part[t, rows(3, 0, half_rows)]], axis=0)
        m1s[t, 1], m1ss[t, 1] = coded(down)
        send_y(m1s, m1r, m1ss, m1sr, 4, m1_recv, t)

    def combine(t):
        await_bytes(m1_recv.at[t], units(260))
        above, below = plain(m1r[t, 0], m1sr[t, 0]), plain(m1r[t, 1], m1sr[t, 1])
        m2s[t, 0], m2ss[t, 0] = coded(part[t, rows(1, 0, half_rows)] + above[A])
        m2s[t, 1], m2ss[t, 1] = coded(part[t, rows(3, half_rows, half_rows)] + below[A])
        send_y(m2s, m2r, m2ss, m2sr, 6, m2_recv, t)
        part[t, rows(0, half_rows, half_rows)] += above[B]
        part[t, rows(0, 0, half_rows)] += below[B]

    def cross(t):
        await_bytes(m2_recv.at[t], units(132))
        part[t, rows(0, 0, half_rows)] += plain(m2r[t, 0], m2sr[t, 0])
        part[t, rows(0, half_rows, half_rows)] += plain(m2r[t, 1], m2sr[t, 1])
        xs[t], xss[t] = coded(part[t, rows(0), pl.ds(pl.multiple_of((1 - x) * HALF, HALF), HALF)])
        remote(xs.at[t], xr.at[t], sent.at[8], x_recv.at[t], to_x).start()
        remote(xss.at[t], xsr.at[t], sent.at[9], x_recv.at[t], to_x).start()

    def crossed(t):
        await_bytes(x_recv.at[t], units(65))
        return part[t, rows(0), pl.ds(pl.multiple_of(x * HALF, HALF), HALF)] + plain(xr[t], xsr[t])

    def travel(t):
        @pl.when(t == 0)
        def _():
            here = crossed(0)
            zs[0, A], zss[0] = coded(here[A])
            send_z(0, 1, 0, half_rows)
            zs[1, B], zss[1] = coded(here[B])
            send_z(1, -1, half_rows, half_rows)

        @pl.when(t == 1)
        def _():
            here = crossed(1)
            await_bytes(z_recv.at[0], units(33))
            zs[2], zss[2] = coded(jnp.concatenate([here[A] + plain(zr[0, A], zsr[0]), here[B]], axis=0))
            send_z(2, 1)

        @pl.when(t == 2)
        def _():
            here = crossed(2)
            await_bytes(z_recv.at[1], units(33))
            zs[3], zss[3] = coded(jnp.concatenate([here[A], here[B] + plain(zr[1, B], zsr[1])], axis=0))
            send_z(3, -1)

        for way in (1, -1):

            @pl.when((t >= 3) & (t <= 6) & (t % 2 == (1 if way == 1 else 0)))
            def _():
                here = crossed(t)
                await_bytes(z_recv.at[t - 1], units(65))
                zs[t + 1], zss[t + 1] = coded(here + plain(zr[t - 1], zsr[t - 1]))
                send_z(t + 1, way)

        @pl.when(t == 7)
        def _():
            here = crossed(7)
            for j in (6, 7):
                await_bytes(z_recv.at[j], units(65))
                here += plain(zr[j], zsr[j])
            fin[core * 4 + y], fin_scale[core * 4 + y] = coded(here)

    def weights(i):
        both = (1, -1)
        for flow, k, now in ((0, i // 2 + 1, i % 2 == 0), (1, i // 2, (i % 2 == 0) & (i > 0)), (2, (i + 1) // 2, i % 2 == 1)):

            @pl.when(now & (k < 4))
            def _():
                ring_events(flow, k, both)

            @pl.when(now & (k == 4))
            def _():
                ring_events(flow, 4, tuple(way for way in both if HOPS[way][flow] == 4))

    def weights_across(i):
        @pl.when(i == 1)
        def _():
            x_events(0, (1,))

        @pl.when((i % 2 == 1) & (i >= 3) & (i <= 7))
        def _():
            x_events((i - 1) // 2, (1, -1))

    def adam(t):
        at = pl.ds(pl.multiple_of(t * QUARTER, QUARTER), QUARTER)
        gradient, master, moment, second = (key_buf[i, at] for i in range(4))
        count = jnp.full((1, HALF), steps[0], I32).astype(F32)
        moment_new = 0.9 * moment + 0.1 * gradient
        second_new = 0.95 * second + 0.05 * gradient * gradient
        first_fix = 1.0 - jnp.exp(count * LOG_KEEP_FIRST)
        second_fix = 1.0 - jnp.exp(count * LOG_KEEP_SECOND)
        key_out[0, at] = moment_new
        key_out[1, at] = second_new
        key_out[2, at] = moment_new / first_fix / (jnp.sqrt(second_new / second_fix) + 1e-08) + 0.1 * master

    def product(i):
        zo = ring(z + jnp.where(i % 2 == 1, (i + 1) // 2, -(i // 2)), Z)

        @pl.when(i == 0)
        def _():
            await_bytes(w_pair_recv.at[zo], w.at[pl.ds(0, HALF)])

        @pl.when(i > 0)
        def _():
            await_bytes(w_pair_recv.at[zo], w.at[pl.ds(0, 2 * HALF)])

        for xo in range(2):
            at = pl.ds(pl.multiple_of((zo * 2 + xo) * 2 * HALF, 2 * HALF), 2 * HALF)
            input_grad[:, at] = lax.dot_general(
                cot[...], w[at], (((1,), (1,)), ((), ())), preferred_element_type=F32
            ).astype(BF16)

    def loop(first, last, body):
        def step(i, carry):
            body(i)
            return carry

        lax.fori_loop(first, last, step, 0)

    def step(i):
        @pl.when(i < Z)
        def _():
            combine(i)

        @pl.when(i + AHEAD < Z)
        def _():
            multiply_own(i + AHEAD)
            multiply(i + AHEAD)

        @pl.when((i >= CROSS_LAG) & (i < CROSS_LAG + Z))
        def _():
            cross(i - CROSS_LAG)

        @pl.when(i >= TRAVEL_LAG)
        def _():
            travel(i - TRAVEL_LAG)

        @pl.when((i >= WEIGHT_LAG) & (i <= WEIGHT_LAG + Z))
        def _():
            weights(i - WEIGHT_LAG)
            weights_across(i - WEIGHT_LAG)

        @pl.when(i < Z)
        def _():
            adam(i)

        @pl.when(i == 4)
        def _():
            product(0)

        @pl.when((i == 6) | (i == 7))
        def _():
            product(i - 5)

    loop(0, AHEAD, multiply_own)
    pair_g.wait_recv()
    turned_g(1)
    loop(0, AHEAD, multiply)
    await_bytes(one.at[8], key_buf)
    own_w.wait()
    arrive(ACROSS, 0, 1)
    for way in (1, -1):
        ring_send(1, way, 0)
    pair_send(z, 1 - x, 0)
    own_cot.wait()
    pair_cot.wait_recv()
    loop(0, TRAVEL_LAG + Z, step)

    def send_fin(at, send, recv, device):
        remote(fin.at[at], fin.at[at], sent.at[send], recv, device).start()
        remote(fin_scale.at[at], fin_scale.at[at], sent.at[send + 1], recv, device).start()

    for r in (2, 1, 3):
        send_fin(core * 4 + y, 12, f_recv.at[r], to_y(r))
    send_fin(core * 4 + y, 14, f_recv.at[0], to_pair)
    x_events(4, (1,))
    loop(3, Z, product)
    for r in (1, 3, 2):
        await_bytes(f_recv.at[r], units(65))
        send_fin(core * 4 + ring(y - r, Y), 14, f_recv.at[0], to_pair)

    pair_cot.wait_send()
    pair_g.wait_send()
    await_bytes(sent.at[0], a_par)
    await_bytes(sent.at[1], w.at[pl.ds(0, 14 * SPLIT + 7 * (HALF - SPLIT))])
    await_bytes(sent.at[2], w.at[pl.ds(0, SPLIT + Z * (HALF - SPLIT))])
    await_bytes(sent.at[3], w.at[pl.ds(0, (2 * Z - 1) * HALF)])
    for i, ref in enumerate((m1s, m1ss, m2s, m2ss, xs, xss, zs.at[pl.ds(0, Z - 1)], zss)):
        await_bytes(sent.at[4 + i], ref)
    for i, ref in enumerate((fin.at[pl.ds(0, 3)], fin_scale.at[pl.ds(0, 3)], fin.at[pl.ds(0, 4)], fin_scale.at[pl.ds(0, 4)])):
        await_bytes(sent.at[12 + i], ref)
    await_bytes(f_recv.at[0], units(260))


def gathered(steps, acts, g, pv, pc, keys):
    dma = pltpu.SemaphoreType.DMA
    hbm, vmem = pl.BlockSpec(memory_space=pltpu.HBM), pl.BlockSpec(memory_space=pltpu.VMEM)
    in_hbm = [pltpu.with_memory_space_constraint(v, pltpu.HBM) for v in (acts, g, pv, pc, *keys)]

    def body(steps, acts, g, pv, pc, k0, k1, k2, k3, *rest):
        exchange(steps, acts, g, pv, pc, (k0, k1, k2, k3), *rest)

    return pl.pallas_call(
        body,
        out_shape=(
            pltpu.VMEM((TOK, FEAT), BF16),
            pltpu.VMEM((3, 1024, 256), F32),
            pltpu.VMEM((8, QUARTER, HALF), I16),
            pltpu.VMEM((8, 1, HALF), F32),
        ),
        in_specs=[pl.BlockSpec(memory_space=pltpu.SMEM)] + [hbm] * 8,
        out_specs=(vmem,) * 4,
        scratch_shapes=[
            pltpu.VMEM((FEAT, COLS), BF16),
            pltpu.VMEM((TOK, COLS), BF16),
            pltpu.VMEM((4, 1024, 256), F32),
            pltpu.VMEM((Z, TOK, 2 * HALF), BF16),
            pltpu.VMEM((Z, TOK, 2 * HALF), BF16),
            pltpu.VMEM((2, TOK, COLS), BF16),
            pltpu.VMEM((COLS, 2 * TOK), BF16),
            pltpu.VMEM((Z, COLS, 2 * HALF), F32),
            *[pltpu.VMEM((Z, 2, QUARTER, 2 * HALF), I16)] * 2,
            *[pltpu.VMEM((Z, 2, 1, 2 * HALF), F32)] * 2,
            *[pltpu.VMEM((Z, 2, QUARTER // 2, 2 * HALF), I16)] * 2,
            *[pltpu.VMEM((Z, 2, 1, 2 * HALF), F32)] * 2,
            *[pltpu.VMEM((Z, QUARTER, HALF), I16)] * 2,
            *[pltpu.VMEM((Z, 1, HALF), F32)] * 2,
            *[pltpu.VMEM((Z, QUARTER, HALF), I16)] * 2,
            *[pltpu.VMEM((Z, 1, HALF), F32)] * 2,
            pltpu.VMEM((260, 1, HALF), F32),
            dma((9,)), dma((Z,)), dma((18,)), dma((Z,)), dma((16,)),
            dma((Z,)), dma((Z,)), dma((Z,)), dma((Z,)), dma((Y,)),
        ],
        compiler_params=pltpu.CompilerParams(
            collective_id=1, has_side_effects=True, vmem_limit_bytes=44 << 20
        ),
    )(steps, *in_hbm)


def write_out(input_grad, key_out, fin, fin_scale, value_to, moment_to, second_to, update_to, input_to, value_grad, sems):
    copies = [
        pltpu.make_async_copy(input_grad.at[pl.ds(i * 64, 64)], input_to.at[pl.ds(i * 64, 64)], sems.at[i])
        for i in range(4)
    ]
    for i, to in enumerate((moment_to, second_to, update_to)):
        copies.append(pltpu.make_async_copy(key_out.at[i], to, sems.at[4 + i]))
    for copy in copies:
        copy.start()
    for core in range(2):
        for y in range(Y):
            value_grad[core * HALF : (core + 1) * HALF, y * QUARTER : (y + 1) * QUARTER] = plain(
                fin[core * 4 + y], fin_scale[core * 4 + y]
            ).T
    last = pltpu.make_async_copy(value_grad, value_to, sems.at[7])
    last.start()
    for copy in copies:
        copy.wait()
    last.wait()


def written(arrays):
    S = jax.ShapeDtypeStruct
    key = S((1024, 256), F32)
    return pl.pallas_call(
        write_out,
        out_shape=(S((2 * HALF, COLS), F32), key, key, key, S((TOK, FEAT), BF16)),
        in_specs=[pl.BlockSpec(memory_space=pltpu.VMEM)] * 4,
        out_specs=(pl.BlockSpec(memory_space=pltpu.HBM),) * 5,
        scratch_shapes=[pltpu.VMEM((2 * HALF, COLS), F32), pltpu.SemaphoreType.DMA((8,))],
        compiler_params=pltpu.CompilerParams(vmem_limit_bytes=8 << 20),
    )(*[pltpu.with_memory_space_constraint(v, pltpu.VMEM) for v in arrays])


def local(
    activations,
    value_cotangent,
    key_gradient,
    key_master,
    key_moment,
    key_second,
    step_count,
    previous_value,
    previous_cotangent,
):
    keys = (key_gradient, key_master, key_moment, key_second)
    return tuple(written(gathered(
        step_count, activations, value_cotangent, previous_value, previous_cotangent, keys
    )))


def solution(mesh):
    in_specs = (
        P(("shard", "replica"), "tensor"),
        P(("shard", "replica"), None),
        P("shard", "tensor"),
        P("shard", "tensor"),
        P("shard", "tensor"),
        P("shard", "tensor"),
        P(),
        P(("tensor", "shard"), None),
        P(("shard", "replica"), "tensor"),
    )
    out_specs = (
        P(("tensor", "shard"), None),
        P("shard", "tensor"),
        P("shard", "tensor"),
        P("shard", "tensor"),
        P(("shard", "replica"), "tensor"),
    )
    return jax.shard_map(local, mesh=mesh, in_specs=in_specs, out_specs=out_specs, check_vma=False)
```

```python
import functools
import math

import jax
import jax.numpy as jnp
from jax import lax
from jax.experimental import pallas as pl
from jax.experimental.pallas import tpu as pltpu
from jax.sharding import PartitionSpec as P

MESH = pl.DeviceIdType.MESH
F32, BF16, I16, I32 = jnp.float32, jnp.bfloat16, jnp.int16, jnp.int32
Z, Y = 8, 4
TOK, FEAT, COLS = 256, 8192, 512
HALF = 256
QUARTER = COLS // Y
EARLY = 6
SPLIT = 192
PARTS = ((0, SPLIT), (SPLIT, HALF - SPLIT))
ACROSS = 12
LOG_KEEP_FIRST, LOG_KEEP_SECOND = math.log(0.9), math.log(0.95)
HOPS = {1: (4, 3, 4), -1: (3, 4, 3)}


def coded(x):
    top = jnp.maximum(jnp.max(jnp.abs(x), axis=0, keepdims=True), 1e-30)
    return jnp.round(x * (32767.0 / top)).astype(I32).astype(I16), top * (1.0 / 32767.0)


def plain(q, scale):
    return q.astype(I32).astype(F32) * scale


def exchange(
    steps, acts, g, pv, pc, key_in,
    input_grad, key_out, fin, fin_scale,
    w, cot, relay, key_buf, a_own, a_par, g_buf, g_t, part,
    m1s, m1r, m1ss, m1sr, m2s, m2r, m2ss, m2sr,
    xs, xr, xss, xsr, zs, zr, zss, zsr,
    n1s, n1r, n1ss, n1sr, n2s, n2r, n2ss, n2sr, es, er, ess, esr, tally,
    one, a_recv, w_recv, w_pair_recv, sent, m1_recv, m2_recv, x_recv, z_recv, f_recv,
):
    tensor = lax.axis_index("tensor")
    shard = lax.axis_index("shard")
    replica = lax.axis_index("replica")
    z, x = shard // 2, shard % 2
    y, core = replica // 2, replica % 2
    sgn = 1 - 2 * core

    def ring(at, n):
        return lax.rem(at + 2 * n, n)

    to_pair = (tensor, shard, y * 2 + 1 - core)
    to_x = (tensor, z * 2 + 1 - x, replica)
    to_next = (1 - tensor, z * 2 + 1 - x, replica)

    def to_y(r):
        return (tensor, shard, ring(y + r, Y) * 2 + core)

    def to_z(way):
        return (tensor, ring(z + way * sgn, Z) * 2 + x, replica)

    def remote(src, dst, send, recv, device):
        return pltpu.make_async_remote_copy(
            src_ref=src, dst_ref=dst, send_sem=send, recv_sem=recv, device_id=device, device_id_type=MESH
        )

    def await_bytes(sem, *refs):
        for ref in refs:
            pltpu.make_async_copy(ref, ref, sem).wait()

    def units(n):
        return tally.at[pl.ds(0, n)]

    barrier = pltpu.get_barrier_semaphore()
    peers = (to_pair, to_x, to_next, to_y(1), to_y(2), to_y(3), to_z(1), to_z(-1))
    for peer in peers:
        pl.semaphore_signal(barrier, inc=1, device_id=peer, device_id_type=MESH)

    def columns(t, b, of_core):
        far = Z // 2 - (t + 1) // 2
        offset = jnp.where(t % 2 == 1, far, -far) * (1 - 2 * of_core)
        start = (ring(z + offset, Z) * 2 + b) * 2 * HALF + of_core * HALF
        return pl.ds(pl.multiple_of(start, HALF), HALF)

    def start_own(t, carry):
        for b in range(2):
            to = a_own.at[t, :, pl.ds(b * HALF, HALF)]
            pltpu.make_async_copy(acts.at[:, columns(t, b, core)], to, one.at[0]).start()
        return carry

    def start_pair(t, carry):
        for b in range(2):
            to = a_par.at[t, :, pl.ds(b * HALF, HALF)]
            remote(acts.at[:, columns(t, b, 1 - core)], to, sent.at[0], a_recv.at[t], to_pair).start()
        return carry

    own_g = pltpu.make_async_copy(g, g_buf.at[0], one.at[1])
    pair_g = remote(g, g_buf.at[1], one.at[2], one.at[3], to_pair)
    own_w = pltpu.make_async_copy(pv, w.at[pl.ds(pl.multiple_of(shard * 2 * HALF, 2 * HALF), 2 * HALF)], one.at[4])
    cot_at = cot.at[:, pl.ds(pl.multiple_of(tensor * 256, 256), 256)]
    own_cot = pltpu.make_async_copy(pc, cot_at, one.at[5])
    next_cot = remote(pc, relay, one.at[6], one.at[7], to_next)
    far_cot = remote(relay, cot.at[:, pl.ds(pl.multiple_of((1 - tensor) * 256, 256), 256)], one.at[9], one.at[10], to_x)

    def block(zo, xo, half):
        first, count = PARTS[half]
        return w.at[pl.ds(pl.multiple_of((zo * 2 + xo) * 2 * HALF + core * HALF + first, 16), count)]

    def own_block(half):
        first, count = PARTS[half]
        return pv.at[pl.ds(pl.multiple_of(core * HALF + first, 16), count)]

    def flow_of(flow):
        return (1 - x if flow == 1 else x), (1 if flow == 2 else 0)

    def origin(way, k):
        return ring(z - way * sgn * k, Z)

    def ring_send(flow, way, k, source=None):
        xo, half = flow_of(flow)
        at = block(origin(way, k), xo, half)
        remote(at if source is None else source, at, sent.at[1], w_recv.at[flow * 4 + k], to_z(way)).start()

    def x_send(zo, half, mark, source=None):
        at = block(zo, x, half)
        remote(at if source is None else source, at, sent.at[2], w_recv.at[mark], to_x).start()

    def pair_send(zo, xo, half):
        at = block(zo, xo, half)
        remote(at, at, sent.at[3], w_pair_recv.at[zo], to_pair).start()

    def arrive(mark, half, count):
        await_bytes(w_recv.at[mark], w.at[pl.ds(0, count * PARTS[half][1])])

    def ring_events(flow, k, ways):
        xo, half = flow_of(flow)
        arrive(flow * 4 + k - 1, half, len(ways))
        for way in ways:
            if k < HOPS[way][flow]:
                ring_send(flow, way, k)

        for way in ways:
            zo = origin(way, k)
            if flow == 2:
                x_send(zo, half, ACROSS + 1 + k)
            pair_send(zo, xo, half)

    def x_events(k, ways):
        arrive(ACROSS + 1 + k, 1, len(ways))
        for way in ways:
            pair_send(origin(way, k), 1 - x, 1)

    def turned_g(b):
        for r in range(Y):
            take = pl.ds(pl.multiple_of(ring(y + r, Y) * QUARTER, QUARTER), QUARTER)
            g_t[r * QUARTER : (r + 1) * QUARTER, b * TOK : (b + 1) * TOK] = (
                g_buf[b, :, take].astype(F32).T.astype(BF16)
            )

    own_g.start()
    lax.fori_loop(0, Z, start_own, 0)
    pl.semaphore_wait(barrier, len(peers))
    pair_g.start()
    lax.fori_loop(0, 1, start_pair, 0)
    x_send(z, 0, ACROSS, own_block(0))
    for way in (1, -1):
        ring_send(0, way, 0, own_block(0))
    x_send(z, 1, ACROSS + 1, own_block(1))
    for way in (1, -1):
        ring_send(2, way, 0, own_block(1))
    lax.fori_loop(1, Z, start_pair, 0)
    own_w.start()
    own_cot.start()
    for i in range(4):
        pltpu.make_async_copy(key_in[i], key_buf.at[i], one.at[8]).start()
    own_g.wait()
    turned_g(0)
    await_bytes(one.at[0], a_own)

    A, B = slice(0, QUARTER // 2), slice(QUARTER // 2, QUARTER)
    half_rows = QUARTER // 2

    def rows(r, first=0, count=QUARTER):
        return pl.ds(r * QUARTER + first, count)

    def send_y(src, dst, src_scale, dst_scale, send, recv, t):
        for way in range(2):
            to = to_y(1 if way == 0 else 3)
            remote(src.at[t, way], dst.at[t, way], sent.at[send], recv, to).start()
            remote(src_scale.at[t, way], dst_scale.at[t, way], sent.at[send + 1], recv, to).start()

    def send_z(j, way, first=0, count=QUARTER):
        some = pl.ds(first, count)
        remote(zs.at[j, some], zr.at[j, some], sent.at[10], z_recv.at[j], to_z(way)).start()
        remote(zss.at[j], zsr.at[j], sent.at[11], z_recv.at[j], to_z(way)).start()

    def multiply_own(t):
        part[t] = jnp.dot(g_t[:, :TOK], a_own[t], preferred_element_type=F32)

    own_lanes = pl.ds(pl.multiple_of(x * HALF, HALF), HALF)
    other_lanes = pl.ds(pl.multiple_of((1 - x) * HALF, HALF), HALF)
    y_first = (m1s, m1r, m1ss, m1sr, 4), (m2s, m2r, m2ss, m2sr, 6)
    x_first = (n1s, n1r, n1ss, n1sr, 16), (n2s, n2r, n2ss, n2sr, 18)

    def route(t):
        return (*y_first, t, slice(None)) if t < EARLY else (*x_first, t - EARLY, own_lanes)

    def multiply_pair(t):
        await_bytes(a_recv.at[t], a_par.at[t])
        part[t] += jnp.dot(g_t[:, TOK:], a_par[t], preferred_element_type=F32)

    def cross_early(t):
        multiply_own(t)
        multiply_pair(t)
        e = t - EARLY
        for r in range(Y):
            es[e, rows(r)], ess[e, r] = coded(part[t, rows(r), other_lanes])
        remote(es.at[e], er.at[e], sent.at[8], x_recv.at[t], to_x).start()
        remote(ess.at[e], esr.at[e], sent.at[9], x_recv.at[t], to_x).start()

    def send_first(t):
        (src, dst, src_scale, dst_scale, send), _, at, lanes = route(t)
        if t >= EARLY:
            await_bytes(x_recv.at[t], units(260))
            for r in range(Y):
                part[t, rows(r), lanes] += plain(er[at, rows(r)], esr[at, r])
        up = jnp.concatenate([part[t, rows(2, 0, half_rows), lanes], part[t, rows(1, half_rows, half_rows), lanes]], axis=0)
        src[at, 0], src_scale[at, 0] = coded(up)
        down = jnp.concatenate([part[t, rows(2, half_rows, half_rows), lanes], part[t, rows(3, 0, half_rows), lanes]], axis=0)
        src[at, 1], src_scale[at, 1] = coded(down)
        send_y(src, dst, src_scale, dst_scale, send, m1_recv.at[t], at)

    def multiply(t):
        multiply_pair(t)
        send_first(t)

    def combine(t):
        (_, got, _, got_scale, _), (src, dst, src_scale, dst_scale, send), at, lanes = route(t)
        await_bytes(m1_recv.at[t], units(260 if t < EARLY else 130))
        above, below = plain(got[at, 0], got_scale[at, 0]), plain(got[at, 1], got_scale[at, 1])
        src[at, 0], src_scale[at, 0] = coded(part[t, rows(1, 0, half_rows), lanes] + above[A])
        src[at, 1], src_scale[at, 1] = coded(part[t, rows(3, half_rows, half_rows), lanes] + below[A])
        send_y(src, dst, src_scale, dst_scale, send, m2_recv.at[t], at)
        part[t, rows(0, half_rows, half_rows), lanes] += above[B]
        part[t, rows(0, 0, half_rows), lanes] += below[B]

    def cross(t):
        _, (_, got, _, got_scale, _), at, lanes = route(t)
        await_bytes(m2_recv.at[t], units(132 if t < EARLY else 66))
        part[t, rows(0, 0, half_rows), lanes] += plain(got[at, 0], got_scale[at, 0])
        part[t, rows(0, half_rows, half_rows), lanes] += plain(got[at, 1], got_scale[at, 1])
        if t < EARLY:
            xs[t], xss[t] = coded(part[t, rows(0), other_lanes])
            remote(xs.at[t], xr.at[t], sent.at[20], x_recv.at[t], to_x).start()
            remote(xss.at[t], xsr.at[t], sent.at[21], x_recv.at[t], to_x).start()

    def crossed(t):
        here = part[t, rows(0), own_lanes]
        if t < EARLY:
            await_bytes(x_recv.at[t], units(65))
            here += plain(xr[t], xsr[t])
        return here

    def travel(t):
        here = crossed(t)
        if t == 0:
            zs[0, A], zss[0] = coded(here[A])
            send_z(0, 1, 0, half_rows)
            zs[1, B], zss[1] = coded(here[B])
            send_z(1, -1, half_rows, half_rows)
        elif t == 1:
            await_bytes(z_recv.at[0], units(33))
            zs[2], zss[2] = coded(jnp.concatenate([here[A] + plain(zr[0, A], zsr[0]), here[B]], axis=0))
            send_z(2, 1)
        elif t == 2:
            await_bytes(z_recv.at[1], units(33))
            zs[3], zss[3] = coded(jnp.concatenate([here[A], here[B] + plain(zr[1, B], zsr[1])], axis=0))
            send_z(3, -1)
        elif t < 7:
            await_bytes(z_recv.at[t - 1], units(65))
            zs[t + 1], zss[t + 1] = coded(here + plain(zr[t - 1], zsr[t - 1]))
            send_z(t + 1, 1 if t % 2 else -1)
        else:
            for j in (6, 7):
                await_bytes(z_recv.at[j], units(65))
                here += plain(zr[j], zsr[j])
            fin[core * 4 + y], fin_scale[core * 4 + y] = coded(here)

    def weights(flow, k):
        ring_events(flow, k, tuple(way for way in (1, -1) if k <= HOPS[way][flow]))

    def weights_across(k):
        x_events(k, (1, -1) if 0 < k < 4 else (1,))

    def adam(t):
        at = pl.ds(pl.multiple_of(t * QUARTER, QUARTER), QUARTER)
        gradient, master, moment, second = (key_buf[i, at] for i in range(4))
        count = jnp.full((1, HALF), steps[0], I32).astype(F32)
        moment_new = 0.9 * moment + 0.1 * gradient
        second_new = 0.95 * second + 0.05 * gradient * gradient
        first_fix = 1.0 - jnp.exp(count * LOG_KEEP_FIRST)
        second_fix = 1.0 - jnp.exp(count * LOG_KEEP_SECOND)
        key_out[0, at] = moment_new
        key_out[1, at] = second_new
        key_out[2, at] = moment_new / first_fix / (jnp.sqrt(second_new / second_fix) + 1e-08) + 0.1 * master

    def product(i):
        zo = ring(z + jnp.where(i % 2 == 1, (i + 1) // 2, -(i // 2)), Z)

        @pl.when(i == 0)
        def _():
            await_bytes(w_pair_recv.at[zo], w.at[pl.ds(0, HALF)])

        @pl.when(i > 0)
        def _():
            await_bytes(w_pair_recv.at[zo], w.at[pl.ds(0, 2 * HALF)])

        for xo in range(2):
            at = pl.ds(pl.multiple_of((zo * 2 + xo) * 2 * HALF, 2 * HALF), 2 * HALF)
            input_grad[:, at] = lax.dot_general(
                cot[...], w[at], (((1,), (1,)), ((), ())), preferred_element_type=F32
            ).astype(BF16)

    def loop(first, last, body):
        def step(i, carry):
            body(i)
            return carry

        lax.fori_loop(first, last, step, 0)

    loop(0, 3, multiply_own)
    pair_g.wait_recv()
    turned_g(1)
    for t in range(3):
        multiply(t)
    next_cot.start()
    for t in range(EARLY, min(EARLY + 1, Z)):
        cross_early(t)
    await_bytes(one.at[8], key_buf)
    own_w.wait()
    arrive(ACROSS, 0, 1)
    for way in (1, -1):
        ring_send(1, way, 0)
    pair_send(z, 1 - x, 0)
    for t in range(EARLY + 1, Z):
        cross_early(t)

    def start_y(t):
        if t < EARLY:
            multiply_own(t)
            multiply(t)
        else:
            send_first(t)

    combine(0)
    start_y(3)
    weights(0, 1)
    weights(2, 1)
    loop(0, 4, adam)
    combine(1)
    start_y(4)
    weights_across(0)
    next_cot.wait_recv()
    far_cot.start()
    combine(2)
    start_y(5)
    cross(0)
    weights(1, 1)
    loop(4, Z, adam)
    combine(3)
    start_y(6)
    cross(1)
    weights(0, 2)
    weights(2, 2)
    combine(4)
    start_y(7)
    cross(2)
    travel(0)
    weights_across(1)
    own_cot.wait()
    far_cot.wait_recv()
    product(0)
    combine(5)
    cross(3)
    travel(1)
    weights(1, 2)
    combine(6)
    cross(4)
    travel(2)
    weights(0, 3)
    weights(2, 3)
    product(1)
    combine(7)
    cross(5)
    travel(3)
    cross(6)
    travel(4)
    cross(7)
    travel(5)
    travel(6)
    weights(1, 3)
    weights_across(2)
    travel(7)

    def send_fin(at, send, recv, device):
        remote(fin.at[at], fin.at[at], sent.at[send], recv, device).start()
        remote(fin_scale.at[at], fin_scale.at[at], sent.at[send + 1], recv, device).start()

    for r in (2, 1, 3):
        send_fin(core * 4 + y, 12, f_recv.at[r], to_y(r))
    send_fin(core * 4 + y, 14, f_recv.at[0], to_pair)
    product(2)
    weights_across(3)
    loop(3, 5, product)
    weights(0, 4)
    weights(2, 4)
    weights(1, 4)
    loop(5, 7, product)
    for r in (1, 3, 2):
        await_bytes(f_recv.at[r], units(65))
        send_fin(core * 4 + ring(y - r, Y), 14, f_recv.at[0], to_pair)
    weights_across(4)
    product(7)

    next_cot.wait_send()
    far_cot.wait_send()
    pair_g.wait_send()
    await_bytes(sent.at[0], a_par)
    await_bytes(sent.at[1], w.at[pl.ds(0, 14 * SPLIT + 7 * (HALF - SPLIT))])
    await_bytes(sent.at[2], w.at[pl.ds(0, SPLIT + Z * (HALF - SPLIT))])
    await_bytes(sent.at[3], w.at[pl.ds(0, (2 * Z - 1) * HALF)])
    for i, ref in enumerate((m1s, m1ss, m2s, m2ss, es, ess, zs.at[pl.ds(0, Z - 1)], zss)):
        await_bytes(sent.at[4 + i], ref)
    for i, ref in enumerate((n1s, n1ss, n2s, n2ss, xs, xss)):
        await_bytes(sent.at[16 + i], ref)
    for i, ref in enumerate((fin.at[pl.ds(0, 3)], fin_scale.at[pl.ds(0, 3)], fin.at[pl.ds(0, 4)], fin_scale.at[pl.ds(0, 4)])):
        await_bytes(sent.at[12 + i], ref)
    await_bytes(f_recv.at[0], units(260))


def gathered(steps, acts, g, pv, pc, keys):
    dma = pltpu.SemaphoreType.DMA
    hbm, vmem = pl.BlockSpec(memory_space=pltpu.HBM), pl.BlockSpec(memory_space=pltpu.VMEM)
    in_hbm = [pltpu.with_memory_space_constraint(v, pltpu.HBM) for v in (acts, g, pv, pc, *keys)]

    def body(steps, acts, g, pv, pc, k0, k1, k2, k3, *rest):
        exchange(steps, acts, g, pv, pc, (k0, k1, k2, k3), *rest)

    return pl.pallas_call(
        body,
        out_shape=(
            pltpu.VMEM((TOK, FEAT), BF16),
            pltpu.VMEM((3, 1024, 256), F32),
            pltpu.VMEM((8, QUARTER, HALF), I16),
            pltpu.VMEM((8, 1, HALF), F32),
        ),
        in_specs=[pl.BlockSpec(memory_space=pltpu.SMEM)] + [hbm] * 8,
        out_specs=(vmem,) * 4,
        scratch_shapes=[
            pltpu.VMEM((FEAT, COLS), BF16),
            pltpu.VMEM((TOK, COLS), BF16),
            pltpu.VMEM((TOK, COLS // 2), BF16),
            pltpu.VMEM((4, 1024, 256), F32),
            pltpu.VMEM((Z, TOK, 2 * HALF), BF16),
            pltpu.VMEM((Z, TOK, 2 * HALF), BF16),
            pltpu.VMEM((2, TOK, COLS), BF16),
            pltpu.VMEM((COLS, 2 * TOK), BF16),
            pltpu.VMEM((Z, COLS, 2 * HALF), F32),
            *[pltpu.VMEM((EARLY, 2, QUARTER, 2 * HALF), I16)] * 2,
            *[pltpu.VMEM((EARLY, 2, 1, 2 * HALF), F32)] * 2,
            *[pltpu.VMEM((EARLY, 2, QUARTER // 2, 2 * HALF), I16)] * 2,
            *[pltpu.VMEM((EARLY, 2, 1, 2 * HALF), F32)] * 2,
            *[pltpu.VMEM((EARLY, QUARTER, HALF), I16)] * 2,
            *[pltpu.VMEM((EARLY, 1, HALF), F32)] * 2,
            *[pltpu.VMEM((Z, QUARTER, HALF), I16)] * 2,
            *[pltpu.VMEM((Z, 1, HALF), F32)] * 2,
            *[pltpu.VMEM((Z - EARLY, 2, QUARTER, HALF), I16)] * 2,
            *[pltpu.VMEM((Z - EARLY, 2, 1, HALF), F32)] * 2,
            *[pltpu.VMEM((Z - EARLY, 2, QUARTER // 2, HALF), I16)] * 2,
            *[pltpu.VMEM((Z - EARLY, 2, 1, HALF), F32)] * 2,
            *[pltpu.VMEM((Z - EARLY, COLS, HALF), I16)] * 2,
            *[pltpu.VMEM((Z - EARLY, Y, 1, HALF), F32)] * 2,
            pltpu.VMEM((260, 1, HALF), F32),
            dma((11,)), dma((Z,)), dma((18,)), dma((Z,)), dma((22,)),
            dma((Z,)), dma((Z,)), dma((Z,)), dma((Z,)), dma((Y,)),
        ],
        compiler_params=pltpu.CompilerParams(
            collective_id=1, has_side_effects=True, vmem_limit_bytes=44 << 20
        ),
    )(steps, *in_hbm)


def write_out(input_grad, key_out, fin, fin_scale, value_to, moment_to, second_to, update_to, input_to, value_grad, sems):
    copies = [
        pltpu.make_async_copy(input_grad.at[pl.ds(i * 64, 64)], input_to.at[pl.ds(i * 64, 64)], sems.at[i])
        for i in range(4)
    ]
    for i, to in enumerate((moment_to, second_to, update_to)):
        copies.append(pltpu.make_async_copy(key_out.at[i], to, sems.at[4 + i]))
    for copy in copies:
        copy.start()
    for core in range(2):
        for y in range(Y):
            value_grad[core * HALF : (core + 1) * HALF, y * QUARTER : (y + 1) * QUARTER] = plain(
                fin[core * 4 + y], fin_scale[core * 4 + y]
            ).T
    last = pltpu.make_async_copy(value_grad, value_to, sems.at[7])
    last.start()
    for copy in copies:
        copy.wait()
    last.wait()


def written(arrays):
    S = jax.ShapeDtypeStruct
    key = S((1024, 256), F32)
    return pl.pallas_call(
        write_out,
        out_shape=(S((2 * HALF, COLS), F32), key, key, key, S((TOK, FEAT), BF16)),
        in_specs=[pl.BlockSpec(memory_space=pltpu.VMEM)] * 4,
        out_specs=(pl.BlockSpec(memory_space=pltpu.HBM),) * 5,
        scratch_shapes=[pltpu.VMEM((2 * HALF, COLS), F32), pltpu.SemaphoreType.DMA((8,))],
        compiler_params=pltpu.CompilerParams(vmem_limit_bytes=8 << 20),
    )(*[pltpu.with_memory_space_constraint(v, pltpu.VMEM) for v in arrays])


def local(
    activations,
    value_cotangent,
    key_gradient,
    key_master,
    key_moment,
    key_second,
    step_count,
    previous_value,
    previous_cotangent,
):
    keys = (key_gradient, key_master, key_moment, key_second)
    return tuple(written(gathered(
        step_count, activations, value_cotangent, previous_value, previous_cotangent, keys
    )))


def solution(mesh):
    in_specs = (
        P(("shard", "replica"), "tensor"),
        P(("shard", "replica"), None),
        P("shard", "tensor"),
        P("shard", "tensor"),
        P("shard", "tensor"),
        P("shard", "tensor"),
        P(),
        P(("tensor", "shard"), None),
        P(("shard", "replica"), "tensor"),
    )
    out_specs = (
        P(("tensor", "shard"), None),
        P("shard", "tensor"),
        P("shard", "tensor"),
        P("shard", "tensor"),
        P(("shard", "replica"), "tensor"),
    )
    return jax.shard_map(local, mesh=mesh, in_specs=in_specs, out_specs=out_specs, check_vma=False)
```

```python
import functools
import math

import jax
import jax.numpy as jnp
from jax import lax
from jax.experimental import pallas as pl
from jax.experimental.pallas import tpu as pltpu
from jax.sharding import PartitionSpec as P

MESH = pl.DeviceIdType.MESH
F32, BF16, I16, I32 = jnp.float32, jnp.bfloat16, jnp.int16, jnp.int32
Z, Y = 8, 4
TOK, FEAT, COLS = 256, 8192, 512
HALF = 256
QUARTER = COLS // Y
EARLY = 6
SPLIT = 192
PARTS = ((0, SPLIT), (SPLIT, HALF - SPLIT))
ACROSS = 12
LOG_KEEP_FIRST, LOG_KEEP_SECOND = math.log(0.9), math.log(0.95)
HOPS = {1: (4, 3, 4), -1: (3, 4, 3)}


def coded(x):
    top = jnp.maximum(jnp.max(jnp.abs(x), axis=0, keepdims=True), 1e-30)
    return jnp.round(x * (32767.0 / top)).astype(I32).astype(I16), top * (1.0 / 32767.0)


def plain(q, scale):
    return q.astype(I32).astype(F32) * scale


def exchange(
    steps, acts, g, pv, pc, key_in,
    input_grad, key_out, fin, fin_scale,
    w, cot, relay, key_buf, a_own, a_par, g_buf, g_t, part,
    m1s, m1r, m1ss, m1sr, m2s, m2r, m2ss, m2sr,
    xs, xr, xss, xsr, zs, zr, zss, zsr,
    n1s, n1r, n1ss, n1sr, n2s, n2r, n2ss, n2sr, es, er, ess, esr, tally,
    one, a_recv, w_recv, w_pair_recv, sent, m1_recv, m2_recv, x_recv, z_recv, f_recv,
):
    tensor = lax.axis_index("tensor")
    shard = lax.axis_index("shard")
    replica = lax.axis_index("replica")
    z, x = shard // 2, shard % 2
    y, core = replica // 2, replica % 2
    sgn = 1 - 2 * core

    def ring(at, n):
        return lax.rem(at + 2 * n, n)

    to_pair = (tensor, shard, y * 2 + 1 - core)
    to_x = (tensor, z * 2 + 1 - x, replica)
    to_next = (1 - tensor, z * 2 + 1 - x, replica)

    def to_y(r):
        return (tensor, shard, ring(y + r, Y) * 2 + core)

    def to_z(way):
        return (tensor, ring(z + way * sgn, Z) * 2 + x, replica)

    def remote(src, dst, send, recv, device):
        return pltpu.make_async_remote_copy(
            src_ref=src, dst_ref=dst, send_sem=send, recv_sem=recv, device_id=device, device_id_type=MESH
        )

    def await_bytes(sem, *refs):
        for ref in refs:
            pltpu.make_async_copy(ref, ref, sem).wait()

    def units(n):
        return tally.at[pl.ds(0, n)]

    barrier = pltpu.get_barrier_semaphore()
    peers = (to_pair, to_x, to_next, to_y(1), to_y(2), to_y(3), to_z(1), to_z(-1))
    for peer in peers:
        pl.semaphore_signal(barrier, inc=1, device_id=peer, device_id_type=MESH)

    def columns(t, b, of_core):
        far = Z // 2 - (t + 1) // 2
        offset = jnp.where(t % 2 == 1, far, -far) * (1 - 2 * of_core)
        start = (ring(z + offset, Z) * 2 + b) * 2 * HALF + of_core * HALF
        return pl.ds(pl.multiple_of(start, HALF), HALF)

    def start_own(t, carry):
        for b in range(2):
            to = a_own.at[t, :, pl.ds(b * HALF, HALF)]
            pltpu.make_async_copy(acts.at[:, columns(t, b, core)], to, one.at[0]).start()
        return carry

    def start_pair(t, carry):
        for b in range(2):
            to = a_par.at[t, :, pl.ds(b * HALF, HALF)]
            remote(acts.at[:, columns(t, b, 1 - core)], to, sent.at[0], a_recv.at[t], to_pair).start()
        return carry

    own_g = pltpu.make_async_copy(g, g_buf.at[0], one.at[1])
    pair_g = remote(g, g_buf.at[1], one.at[2], one.at[3], to_pair)
    own_w = pltpu.make_async_copy(pv, w.at[pl.ds(pl.multiple_of(shard * 2 * HALF, 2 * HALF), 2 * HALF)], one.at[4])
    cot_at = cot.at[:, pl.ds(pl.multiple_of(tensor * 256, 256), 256)]
    own_cot = pltpu.make_async_copy(pc, cot_at, one.at[5])
    next_cot = remote(pc, relay, one.at[6], one.at[7], to_next)
    far_cot = remote(relay, cot.at[:, pl.ds(pl.multiple_of((1 - tensor) * 256, 256), 256)], one.at[9], one.at[10], to_x)

    def block(zo, xo, half):
        first, count = PARTS[half]
        return w.at[pl.ds(pl.multiple_of((zo * 2 + xo) * 2 * HALF + core * HALF + first, 16), count)]

    def own_block(half):
        first, count = PARTS[half]
        return pv.at[pl.ds(pl.multiple_of(core * HALF + first, 16), count)]

    def flow_of(flow):
        return (1 - x if flow == 1 else x), (1 if flow == 2 else 0)

    def origin(way, k):
        return ring(z - way * sgn * k, Z)

    def ring_send(flow, way, k, source=None):
        xo, half = flow_of(flow)
        at = block(origin(way, k), xo, half)
        remote(at if source is None else source, at, sent.at[1], w_recv.at[flow * 4 + k], to_z(way)).start()

    def x_send(zo, half, mark, source=None):
        at = block(zo, x, half)
        remote(at if source is None else source, at, sent.at[2], w_recv.at[mark], to_x).start()

    def pair_send(zo, xo, half):
        at = block(zo, xo, half)
        remote(at, at, sent.at[3], w_pair_recv.at[zo], to_pair).start()

    def arrive(mark, half, count):
        await_bytes(w_recv.at[mark], w.at[pl.ds(0, count * PARTS[half][1])])

    def ring_events(flow, k, ways):
        xo, half = flow_of(flow)
        arrive(flow * 4 + k - 1, half, len(ways))
        for way in ways:
            if k < HOPS[way][flow]:
                ring_send(flow, way, k)

        for way in ways:
            zo = origin(way, k)
            if flow == 2:
                x_send(zo, half, ACROSS + 1 + k)
            pair_send(zo, xo, half)

    def x_events(k, ways):
        arrive(ACROSS + 1 + k, 1, len(ways))
        for way in ways:
            pair_send(origin(way, k), 1 - x, 1)

    def turned_g(b):
        for r in range(Y):
            take = pl.ds(pl.multiple_of(ring(y + r, Y) * QUARTER, QUARTER), QUARTER)
            g_t[r * QUARTER : (r + 1) * QUARTER, b * TOK : (b + 1) * TOK] = (
                g_buf[b, :, take].astype(F32).T.astype(BF16)
            )

    own_g.start()
    lax.fori_loop(0, Z, start_own, 0)
    pl.semaphore_wait(barrier, len(peers))
    pair_g.start()
    lax.fori_loop(0, 1, start_pair, 0)
    x_send(z, 0, ACROSS, own_block(0))
    for way in (1, -1):
        ring_send(0, way, 0, own_block(0))
    x_send(z, 1, ACROSS + 1, own_block(1))
    for way in (1, -1):
        ring_send(2, way, 0, own_block(1))
    lax.fori_loop(1, Z, start_pair, 0)
    own_w.start()
    own_cot.start()
    for i in range(4):
        pltpu.make_async_copy(key_in[i], key_buf.at[i], one.at[8]).start()
    own_g.wait()
    turned_g(0)
    await_bytes(one.at[0], a_own)

    A, B = slice(0, QUARTER // 2), slice(QUARTER // 2, QUARTER)
    half_rows = QUARTER // 2

    def rows(r, first=0, count=QUARTER):
        return pl.ds(r * QUARTER + first, count)

    def send_y(src, dst, src_scale, dst_scale, send, recv, t):
        for way in range(2):
            to = to_y(1 if way == 0 else 3)
            remote(src.at[t, way], dst.at[t, way], sent.at[send], recv, to).start()
            remote(src_scale.at[t, way], dst_scale.at[t, way], sent.at[send + 1], recv, to).start()

    def send_z(j, way, first=0, count=QUARTER):
        some = pl.ds(first, count)
        remote(zs.at[j, some], zr.at[j, some], sent.at[10], z_recv.at[j], to_z(way)).start()
        remote(zss.at[j], zsr.at[j], sent.at[11], z_recv.at[j], to_z(way)).start()

    def multiply_own(t):
        part[t] = jnp.dot(g_t[:, :TOK], a_own[t], preferred_element_type=F32)

    own_lanes = pl.ds(pl.multiple_of(x * HALF, HALF), HALF)
    other_lanes = pl.ds(pl.multiple_of((1 - x) * HALF, HALF), HALF)
    y_first = (m1s, m1r, m1ss, m1sr, 4), (m2s, m2r, m2ss, m2sr, 6)
    x_first = (n1s, n1r, n1ss, n1sr, 16), (n2s, n2r, n2ss, n2sr, 18)

    def route(t):
        return (*y_first, t, slice(None)) if t < EARLY else (*x_first, t - EARLY, own_lanes)

    def multiply_pair(t):
        await_bytes(a_recv.at[t], a_par.at[t])
        part[t] += jnp.dot(g_t[:, TOK:], a_par[t], preferred_element_type=F32)

    def cross_early(t):
        multiply_own(t)
        multiply_pair(t)
        e = t - EARLY
        for r in range(Y):
            es[e, rows(r)], ess[e, r] = coded(part[t, rows(r), other_lanes])
        remote(es.at[e], er.at[e], sent.at[8], x_recv.at[t], to_x).start()
        remote(ess.at[e], esr.at[e], sent.at[9], x_recv.at[t], to_x).start()

    def send_first(t):
        (src, dst, src_scale, dst_scale, send), _, at, lanes = route(t)
        if t >= EARLY:
            await_bytes(x_recv.at[t], units(260))
            for r in range(Y):
                part[t, rows(r), lanes] += plain(er[at, rows(r)], esr[at, r])
        up = jnp.concatenate([part[t, rows(2, 0, half_rows), lanes], part[t, rows(1, half_rows, half_rows), lanes]], axis=0)
        src[at, 0], src_scale[at, 0] = coded(up)
        down = jnp.concatenate([part[t, rows(2, half_rows, half_rows), lanes], part[t, rows(3, 0, half_rows), lanes]], axis=0)
        src[at, 1], src_scale[at, 1] = coded(down)
        send_y(src, dst, src_scale, dst_scale, send, m1_recv.at[t], at)

    def multiply(t):
        multiply_pair(t)
        send_first(t)

    def combine(t):
        (_, got, _, got_scale, _), (src, dst, src_scale, dst_scale, send), at, lanes = route(t)
        await_bytes(m1_recv.at[t], units(260 if t < EARLY else 130))
        above, below = plain(got[at, 0], got_scale[at, 0]), plain(got[at, 1], got_scale[at, 1])
        src[at, 0], src_scale[at, 0] = coded(part[t, rows(1, 0, half_rows), lanes] + above[A])
        src[at, 1], src_scale[at, 1] = coded(part[t, rows(3, half_rows, half_rows), lanes] + below[A])
        send_y(src, dst, src_scale, dst_scale, send, m2_recv.at[t], at)
        part[t, rows(0, half_rows, half_rows), lanes] += above[B]
        part[t, rows(0, 0, half_rows), lanes] += below[B]

    def cross(t):
        _, (_, got, _, got_scale, _), at, lanes = route(t)
        await_bytes(m2_recv.at[t], units(132 if t < EARLY else 66))
        part[t, rows(0, 0, half_rows), lanes] += plain(got[at, 0], got_scale[at, 0])
        part[t, rows(0, half_rows, half_rows), lanes] += plain(got[at, 1], got_scale[at, 1])
        if t < EARLY:
            xs[t], xss[t] = coded(part[t, rows(0), other_lanes])
            remote(xs.at[t], xr.at[t], sent.at[20], x_recv.at[t], to_x).start()
            remote(xss.at[t], xsr.at[t], sent.at[21], x_recv.at[t], to_x).start()

    def crossed(t):
        here = part[t, rows(0), own_lanes]
        if t < EARLY:
            await_bytes(x_recv.at[t], units(65))
            here += plain(xr[t], xsr[t])
        return here

    def travel(t):
        here = crossed(t)
        if t == 0:
            zs[0, A], zss[0] = coded(here[A])
            send_z(0, 1, 0, half_rows)
            zs[1, B], zss[1] = coded(here[B])
            send_z(1, -1, half_rows, half_rows)
        elif t == 1:
            await_bytes(z_recv.at[0], units(33))
            zs[2], zss[2] = coded(jnp.concatenate([here[A] + plain(zr[0, A], zsr[0]), here[B]], axis=0))
            send_z(2, 1)
        elif t == 2:
            await_bytes(z_recv.at[1], units(33))
            zs[3], zss[3] = coded(jnp.concatenate([here[A], here[B] + plain(zr[1, B], zsr[1])], axis=0))
            send_z(3, -1)
        elif t < 7:
            await_bytes(z_recv.at[t - 1], units(65))
            zs[t + 1], zss[t + 1] = coded(here + plain(zr[t - 1], zsr[t - 1]))
            send_z(t + 1, 1 if t % 2 else -1)
        else:
            for j in (6, 7):
                await_bytes(z_recv.at[j], units(65))
                here += plain(zr[j], zsr[j])
            fin[core * 4 + y], fin_scale[core * 4 + y] = coded(here)

    def weights(flow, k):
        ring_events(flow, k, tuple(way for way in (1, -1) if k <= HOPS[way][flow]))

    def weights_across(k):
        x_events(k, (1, -1) if 0 < k < 4 else (1,))

    def adam(t):
        at = pl.ds(pl.multiple_of(t * QUARTER, QUARTER), QUARTER)
        gradient, master, moment, second = (key_buf[i, at] for i in range(4))
        count = jnp.full((1, HALF), steps[0], I32).astype(F32)
        moment_new = 0.9 * moment + 0.1 * gradient
        second_new = 0.95 * second + 0.05 * gradient * gradient
        first_fix = 1.0 - jnp.exp(count * LOG_KEEP_FIRST)
        second_fix = 1.0 - jnp.exp(count * LOG_KEEP_SECOND)
        key_out[0, at] = moment_new
        key_out[1, at] = second_new
        key_out[2, at] = moment_new / first_fix / (jnp.sqrt(second_new / second_fix) + 1e-08) + 0.1 * master

    def product(i):
        zo = ring(z + jnp.where(i % 2 == 1, (i + 1) // 2, -(i // 2)), Z)

        @pl.when(i == 0)
        def _():
            await_bytes(w_pair_recv.at[zo], w.at[pl.ds(0, HALF)])

        @pl.when(i > 0)
        def _():
            await_bytes(w_pair_recv.at[zo], w.at[pl.ds(0, 2 * HALF)])

        for xo in range(2):
            at = pl.ds(pl.multiple_of((zo * 2 + xo) * 2 * HALF, 2 * HALF), 2 * HALF)
            input_grad[:, at] = lax.dot_general(
                cot[...], w[at], (((1,), (1,)), ((), ())), preferred_element_type=F32
            ).astype(BF16)

    def loop(first, last, body):
        def step(i, carry):
            body(i)
            return carry

        lax.fori_loop(first, last, step, 0)

    loop(0, 3, multiply_own)
    pair_g.wait_recv()
    turned_g(1)
    for t in range(3):
        multiply(t)
    next_cot.start()
    for t in range(EARLY, min(EARLY + 1, Z)):
        cross_early(t)
    await_bytes(one.at[8], key_buf)
    own_w.wait()
    arrive(ACROSS, 0, 1)
    for way in (1, -1):
        ring_send(1, way, 0)
    pair_send(z, 1 - x, 0)
    for t in range(EARLY + 1, Z):
        cross_early(t)

    def start_y(t):
        if t < EARLY:
            multiply_own(t)
            multiply(t)
        else:
            send_first(t)

    combine(0)
    start_y(3)
    weights(0, 1)
    weights(2, 1)
    loop(0, 4, adam)
    combine(1)
    start_y(4)
    weights_across(0)
    next_cot.wait_recv()
    far_cot.start()
    combine(2)
    start_y(5)
    cross(0)
    weights(1, 1)
    loop(4, Z, adam)
    combine(3)
    start_y(6)
    cross(1)
    weights(0, 2)
    weights(2, 2)
    combine(4)
    start_y(7)
    cross(2)
    travel(0)
    weights_across(1)
    own_cot.wait()
    far_cot.wait_recv()
    product(0)
    weights(1, 2)
    combine(5)
    cross(3)
    travel(1)
    combine(6)
    weights(0, 3)
    weights(2, 3)
    cross(4)
    travel(2)
    product(1)
    combine(7)
    cross(5)
    travel(3)
    cross(6)
    travel(4)
    cross(7)
    weights(1, 3)
    travel(5)
    travel(6)
    weights_across(2)
    travel(7)

    def send_fin(at, send, recv, device):
        remote(fin.at[at], fin.at[at], sent.at[send], recv, device).start()
        remote(fin_scale.at[at], fin_scale.at[at], sent.at[send + 1], recv, device).start()

    for r in (2, 1, 3):
        send_fin(core * 4 + y, 12, f_recv.at[r], to_y(r))
    send_fin(core * 4 + y, 14, f_recv.at[0], to_pair)
    product(2)
    weights_across(3)
    loop(3, 5, product)
    weights(0, 4)
    weights(2, 4)
    weights(1, 4)
    loop(5, 7, product)
    for r in (1, 3, 2):
        await_bytes(f_recv.at[r], units(65))
        send_fin(core * 4 + ring(y - r, Y), 14, f_recv.at[0], to_pair)
    weights_across(4)
    product(7)

    next_cot.wait_send()
    far_cot.wait_send()
    pair_g.wait_send()
    await_bytes(sent.at[0], a_par)
    await_bytes(sent.at[1], w.at[pl.ds(0, 14 * SPLIT + 7 * (HALF - SPLIT))])
    await_bytes(sent.at[2], w.at[pl.ds(0, SPLIT + Z * (HALF - SPLIT))])
    await_bytes(sent.at[3], w.at[pl.ds(0, (2 * Z - 1) * HALF)])
    for i, ref in enumerate((m1s, m1ss, m2s, m2ss, es, ess, zs.at[pl.ds(0, Z - 1)], zss)):
        await_bytes(sent.at[4 + i], ref)
    for i, ref in enumerate((n1s, n1ss, n2s, n2ss, xs, xss)):
        await_bytes(sent.at[16 + i], ref)
    for i, ref in enumerate((fin.at[pl.ds(0, 3)], fin_scale.at[pl.ds(0, 3)], fin.at[pl.ds(0, 4)], fin_scale.at[pl.ds(0, 4)])):
        await_bytes(sent.at[12 + i], ref)
    await_bytes(f_recv.at[0], units(260))


def gathered(steps, acts, g, pv, pc, keys):
    dma = pltpu.SemaphoreType.DMA
    hbm, vmem = pl.BlockSpec(memory_space=pltpu.HBM), pl.BlockSpec(memory_space=pltpu.VMEM)
    in_hbm = [pltpu.with_memory_space_constraint(v, pltpu.HBM) for v in (acts, g, pv, pc, *keys)]

    def body(steps, acts, g, pv, pc, k0, k1, k2, k3, *rest):
        exchange(steps, acts, g, pv, pc, (k0, k1, k2, k3), *rest)

    return pl.pallas_call(
        body,
        out_shape=(
            pltpu.VMEM((TOK, FEAT), BF16),
            pltpu.VMEM((3, 1024, 256), F32),
            pltpu.VMEM((8, QUARTER, HALF), I16),
            pltpu.VMEM((8, 1, HALF), F32),
        ),
        in_specs=[pl.BlockSpec(memory_space=pltpu.SMEM)] + [hbm] * 8,
        out_specs=(vmem,) * 4,
        scratch_shapes=[
            pltpu.VMEM((FEAT, COLS), BF16),
            pltpu.VMEM((TOK, COLS), BF16),
            pltpu.VMEM((TOK, COLS // 2), BF16),
            pltpu.VMEM((4, 1024, 256), F32),
            pltpu.VMEM((Z, TOK, 2 * HALF), BF16),
            pltpu.VMEM((Z, TOK, 2 * HALF), BF16),
            pltpu.VMEM((2, TOK, COLS), BF16),
            pltpu.VMEM((COLS, 2 * TOK), BF16),
            pltpu.VMEM((Z, COLS, 2 * HALF), F32),
            *[pltpu.VMEM((EARLY, 2, QUARTER, 2 * HALF), I16)] * 2,
            *[pltpu.VMEM((EARLY, 2, 1, 2 * HALF), F32)] * 2,
            *[pltpu.VMEM((EARLY, 2, QUARTER // 2, 2 * HALF), I16)] * 2,
            *[pltpu.VMEM((EARLY, 2, 1, 2 * HALF), F32)] * 2,
            *[pltpu.VMEM((EARLY, QUARTER, HALF), I16)] * 2,
            *[pltpu.VMEM((EARLY, 1, HALF), F32)] * 2,
            *[pltpu.VMEM((Z, QUARTER, HALF), I16)] * 2,
            *[pltpu.VMEM((Z, 1, HALF), F32)] * 2,
            *[pltpu.VMEM((Z - EARLY, 2, QUARTER, HALF), I16)] * 2,
            *[pltpu.VMEM((Z - EARLY, 2, 1, HALF), F32)] * 2,
            *[pltpu.VMEM((Z - EARLY, 2, QUARTER // 2, HALF), I16)] * 2,
            *[pltpu.VMEM((Z - EARLY, 2, 1, HALF), F32)] * 2,
            *[pltpu.VMEM((Z - EARLY, COLS, HALF), I16)] * 2,
            *[pltpu.VMEM((Z - EARLY, Y, 1, HALF), F32)] * 2,
            pltpu.VMEM((260, 1, HALF), F32),
            dma((11,)), dma((Z,)), dma((18,)), dma((Z,)), dma((22,)),
            dma((Z,)), dma((Z,)), dma((Z,)), dma((Z,)), dma((Y,)),
        ],
        compiler_params=pltpu.CompilerParams(
            collective_id=1, has_side_effects=True, vmem_limit_bytes=44 << 20
        ),
    )(steps, *in_hbm)


def write_out(input_grad, key_out, fin, fin_scale, value_to, moment_to, second_to, update_to, input_to, value_grad, sems):
    copies = [
        pltpu.make_async_copy(input_grad.at[pl.ds(i * 64, 64)], input_to.at[pl.ds(i * 64, 64)], sems.at[i])
        for i in range(4)
    ]
    for i, to in enumerate((moment_to, second_to, update_to)):
        copies.append(pltpu.make_async_copy(key_out.at[i], to, sems.at[4 + i]))
    for copy in copies:
        copy.start()
    for core in range(2):
        for y in range(Y):
            value_grad[core * HALF : (core + 1) * HALF, y * QUARTER : (y + 1) * QUARTER] = plain(
                fin[core * 4 + y], fin_scale[core * 4 + y]
            ).T
    last = pltpu.make_async_copy(value_grad, value_to, sems.at[7])
    last.start()
    for copy in copies:
        copy.wait()
    last.wait()


def written(arrays):
    S = jax.ShapeDtypeStruct
    key = S((1024, 256), F32)
    return pl.pallas_call(
        write_out,
        out_shape=(S((2 * HALF, COLS), F32), key, key, key, S((TOK, FEAT), BF16)),
        in_specs=[pl.BlockSpec(memory_space=pltpu.VMEM)] * 4,
        out_specs=(pl.BlockSpec(memory_space=pltpu.HBM),) * 5,
        scratch_shapes=[pltpu.VMEM((2 * HALF, COLS), F32), pltpu.SemaphoreType.DMA((8,))],
        compiler_params=pltpu.CompilerParams(vmem_limit_bytes=8 << 20),
    )(*[pltpu.with_memory_space_constraint(v, pltpu.VMEM) for v in arrays])


def local(
    activations,
    value_cotangent,
    key_gradient,
    key_master,
    key_moment,
    key_second,
    step_count,
    previous_value,
    previous_cotangent,
):
    keys = (key_gradient, key_master, key_moment, key_second)
    return tuple(written(gathered(
        step_count, activations, value_cotangent, previous_value, previous_cotangent, keys
    )))


def solution(mesh):
    in_specs = (
        P(("shard", "replica"), "tensor"),
        P(("shard", "replica"), None),
        P("shard", "tensor"),
        P("shard", "tensor"),
        P("shard", "tensor"),
        P("shard", "tensor"),
        P(),
        P(("tensor", "shard"), None),
        P(("shard", "replica"), "tensor"),
    )
    out_specs = (
        P(("tensor", "shard"), None),
        P("shard", "tensor"),
        P("shard", "tensor"),
        P("shard", "tensor"),
        P(("shard", "replica"), "tensor"),
    )
    return jax.shard_map(local, mesh=mesh, in_specs=in_specs, out_specs=out_specs, check_vma=False)
```
